128 devices in a mesh: pool: 32 (over x, z, core), blk: 4 (over y).
Axes of the slice: x: 4, y: 4, z: 4, core: 2. Of those that a mesh axis runs over, the one named last changes fastest.
Arguments:
- embeddings: float32 [131072, 1024], P(('pool', 'blk')), may hold values from -6 to 6
- cluster_ids: int32 [131072, 1], P(('pool', 'blk')), may hold values from 0 to 127; in each aligned block of 1024 rows (0 to 1023, 1024 to 2047, ...) at most 16 rows name the same one
Outputs:
- density: float32 [131072], P(('pool', 'blk'))
The draws below stay inside these ranges and needn't reach their ends.
Inputs may be any that keep to these rules, and one draw needn't show every extreme that they name: `cluster_ids`: within the rows of one device no cluster appears more than 16 times, and some cluster appears exactly 16 times; every cluster appears in some row.
All inputs are finite; a program needn't handle non-finite values.
Results may differ from the reference program's by a relative error of at most 0.0003.
Values may be sent and summed in bfloat16 or wider, within the bound.
A program may use at most 64 MiB of HBM per device.

```python
import math
import jax
import jax.numpy as jnp
import numpy as np
from jax import lax

D = 1024
ROW_DEV = 1024
ROWS = 131072
CLUSTERS = 128
CAP = 16
N_POOL = 32
N_BLK = 4


def level_of(rng, dims, pieces, smallest, top_value):
    def one(axis_at, blocks):
        heights = jax.random.uniform(jax.random.fold_in(jax.random.fold_in(rng, 6), axis_at), (blocks,), jnp.float32, smallest / len(pieces), top_value / len(pieces))
        return jnp.repeat(jnp.exp(heights), dims[axis_at] // blocks).reshape((-1,) + (1,) * (len(dims) - axis_at - 1))

    factor_of = one(*pieces[0])
    for cut in pieces[1:]:
        factor_of = factor_of * one(*cut)
    return factor_of


def assign_block(own_key, own, number, rows, amount, top, bound, lean):
    ranking = jax.random.permutation(own_key, amount)
    crowded, common = load_shares(amount, rows * top, bound, lean, True), load_shares(amount, rows * top, bound, lean, False)
    places = jnp.arange(amount)

    def named(lengths, rotation):
        used = int((lengths > 0).sum())
        fixed = max(1, used // 4)
        moved = fixed + (places - fixed + rotation * (used - fixed)) % max(1, amount - fixed)
        return jnp.zeros((amount,), jnp.int32).at[ranking[jnp.where(places < fixed, places, moved)]].set(jnp.asarray(lengths, jnp.int32))

    lengths = jnp.where(number % 4 == 0, named(crowded, number // 4), named(common, number - number // 4 - 1))
    mixed = jax.random.permutation(jax.random.fold_in(own, 3), amount)
    source_of, taker = mixed[0:amount // 2 * 2:2], mixed[1:amount // 2 * 2:2]
    margin = jnp.minimum(lengths[source_of] - 1, bound - lengths[taker]) // 2
    margin = jnp.where((source_of == ranking[0]) | (taker == ranking[0]) | (lengths[taker] == 0), 0, jnp.maximum(margin, 0))
    moved = jax.random.randint(jax.random.fold_in(own, 4), (amount // 2,), 0, 1 << 20) % (margin + 1)
    lengths = lengths.at[source_of].add(-moved).at[taker].add(moved)
    items = jnp.searchsorted(jnp.cumsum(lengths), jnp.arange(rows * top), side="right").astype(jnp.int32)
    grid = items.reshape(top, rows).T
    grid = grid[jax.random.permutation(jax.random.fold_in(own, 1), rows)]
    rotation = jax.random.randint(jax.random.fold_in(own, 2), (rows, 1), 0, top)
    return jnp.take_along_axis(grid, (jnp.arange(top)[None, :] + rotation) % top, axis=1)


def load_shares(count, total, bound, slope, full):
    weights = [(1 << 20) // math.isqrt(grade ** slope) + 1 for grade in range(1, count + 1)]
    largest = bound if full else min(bound, max(-(-total // count), total * weights[0] // sum(weights)))
    least = 1 if total - largest >= count - 1 else 0
    counts, spare = [largest] + [least] * (count - 1), total - largest - least * (count - 1)
    while spare > 0:
        movable = [i for i in range(1, count) if counts[i] < largest] or [i for i in range(1, count) if counts[i] < bound]
        whole, remaining = sum([weights[i] for i in movable]), spare
        for i in movable:
            extra = min(bound - counts[i], max(1, remaining * weights[i] // whole), spare)
            counts[i] = counts[i] + extra
            spare = spare - extra
    return np.array(counts)


def noise(stream_key, extent, scale, reach, split=(), kind=jnp.bfloat16):
    drawn = scale * jax.random.normal(stream_key, extent, jnp.float32)
    if split:
        drawn = drawn * level_of(stream_key, extent, split, -0.22, 0.18)
    return jnp.clip(drawn, -reach, reach).astype(kind)


def setup_inputs(seed: int = 0) -> dict:
    key_of = jax.random.split(jax.random.key(seed), 3)
    embeddings = noise(key_of[0], (ROWS, D), 1.0, 6.0, ((0, 128),), jnp.float32)
    cluster_ids_keys = jax.random.split(jax.random.fold_in(key_of[1], 1), ROWS // ROW_DEV)
    cluster_ids_turns = jax.random.permutation(jax.random.fold_in(key_of[1], 3), ROWS // ROW_DEV)
    cluster_ids = jax.vmap(lambda own, number: assign_block(jax.random.fold_in(key_of[1], 2), own, number, ROW_DEV, CLUSTERS, 1, CAP, 2))(cluster_ids_keys, cluster_ids_turns).reshape((ROWS, 1))
    return dict(embeddings=embeddings, cluster_ids=cluster_ids)


SOFTMAX_TEMP = 0.02
EPSILON = 1e-06

def normalized_rows(embeddings):
    squares = lax.optimization_barrier(jnp.sum(embeddings * embeddings, axis=1, keepdims=True))
    return (embeddings * lax.rsqrt(squares + EPSILON)).astype(jnp.bfloat16)

def cluster_density(members, present):
    count = members.shape[0]
    block = 1024 if count % 1024 == 0 else count
    duplicate_flags = present.astype(jnp.float32)

    def one_block(begin):
        queries = lax.dynamic_slice_in_dim(members, begin, block, 0)
        density_scores = lax.dot_general(queries, members, (((1,), (1,)), ((), ())), preferred_element_type=jnp.float32)
        keep_weights = jnp.exp(density_scores / SOFTMAX_TEMP) * duplicate_flags[None, :]
        own = begin + jnp.arange(block, dtype=jnp.int32)[:, None]
        other = jnp.arange(count, dtype=jnp.int32)[None, :]
        keep_weights = jnp.where(own == other, jnp.zeros_like(keep_weights), keep_weights)
        return jnp.log(1.0 + lax.optimization_barrier(jnp.sum(keep_weights, axis=1)))
    starts = jnp.arange(count // block, dtype=jnp.int32) * block
    return lax.map(one_block, starts).reshape(count)

def reference(embeddings, cluster_ids):
    devices = N_POOL * N_BLK
    unit = normalized_rows(embeddings)
    ids = cluster_ids[:, 0].reshape(devices, ROW_DEV)
    onehot = (ids[:, :, None] == jnp.arange(devices, dtype=jnp.int32)[None, None, :]).astype(jnp.int32)
    rank = lax.optimization_barrier(jnp.sum((jnp.cumsum(onehot, axis=1) - onehot) * onehot, axis=2)).astype(jnp.int32)
    source = jnp.arange(devices, dtype=jnp.int32)[:, None]
    slot = (ids * (devices * CAP) + source * CAP + rank).reshape(-1).astype(jnp.int32)
    owner = jnp.zeros((devices * devices * CAP, D), jnp.bfloat16).at[slot].set(unit)
    present = jnp.zeros((devices * devices * CAP,), jnp.bfloat16).at[slot].set(jnp.ones((ROWS,), jnp.bfloat16))
    owner = owner.reshape(devices, devices * CAP, D)
    present = present.reshape(devices, devices * CAP)
    dens = lax.map(lambda pair: cluster_density(pair[0], pair[1]), (owner, present))
    return dens.reshape(-1)[slot]
```

```python
import jax
import jax.numpy as jnp
from jax import lax
from jax.experimental import pallas as pl
from jax.experimental.pallas import tpu as pltpu
from jax.sharding import PartitionSpec as P

EPSILON = 1e-06
SCALE = 50.0 * 1.4426950408889634
MESH = pl.DeviceIdType.MESH
ROWS = 1024
WIDTH = 1024
DEVICES = 128
CAP = 16
SLOTS = DEVICES * CAP
CHUNK = 256
CHUNKS = SLOTS // CHUNK
PER_CHUNK = CHUNK // CAP
STEP = 27
EMPTY = 1.25
NT = (((1,), (1,)), ((), ()))


def offset_of(k):
    v = ((k // 2) * STEP) % 64
    return v // 16, (v // 4) % 4, v % 4, k % 2


def place():
    pool = lax.axis_index("pool")
    return pool // 8, lax.axis_index("blk"), (pool // 2) % 4, pool % 2


def target(me, k):
    a, b, d, f = offset_of(k)
    x, y, z, c = (me[0] + a) % 4, (me[1] + b) % 4, (me[2] + d) % 4, (me[3] + f) % 2
    return x, y, z, c


def device_id(x, y, z, c):
    return ((x * 4 + z) * 2 + c, y)


def cluster_of(x, y, z, c):
    return (y * 2 + c) * 16 + x * 4 + z


def split3(v):
    hi = v.astype(jnp.bfloat16)
    rest = v - hi.astype(jnp.float32)
    mid = rest.astype(jnp.bfloat16)
    lo = (rest - mid.astype(jnp.float32)).astype(jnp.bfloat16)
    return hi, mid, lo


def kernel(
    emb_ref, ids_ref, out_ref,
    unit, send, recv, flags, acc, ret0, ret1, ret2, ret3,
    send_sem, recv_sem, s1_sem, r1_sem, s2_sem, r2_sem,
):
    me = place()
    x, y, z, c = me

    barrier = pltpu.get_barrier_semaphore()

    def greet(k, _):
        pl.semaphore_signal(
            barrier, inc=1, device_id=device_id(*target(me, k)), device_id_type=MESH
        )
        return 0

    lax.fori_loop(1, DEVICES, greet, 0)

    for b in range(4):
        rows = pl.ds(b * 256, 256)
        e = emb_ref[rows, :]
        squares = jnp.sum(e * e, axis=1, keepdims=True)
        unit[rows, :] = (e * lax.rsqrt(squares + EPSILON)).astype(jnp.bfloat16)

    ids = ids_ref[...]
    cluster = lax.broadcasted_iota(jnp.int32, (DEVICES, ROWS), 0)
    onehot = jnp.where(cluster == ids, 1.0, 0.0)
    onehot16 = onehot.astype(jnp.bfloat16)
    upper = jnp.where(
        lax.broadcasted_iota(jnp.int32, (256, 256), 0)
        < lax.broadcasted_iota(jnp.int32, (256, 256), 1),
        1.0, 0.0,
    ).astype(jnp.bfloat16)
    carry = jnp.zeros((DEVICES, 1), jnp.float32)
    ranks = []
    for b in range(4):
        cols = slice(b * 256, (b + 1) * 256)
        before = jnp.dot(onehot16[:, cols], upper, preferred_element_type=jnp.float32) + carry
        ranks.append(jnp.sum(before * onehot[:, cols], axis=0, keepdims=True))
        carry = before[:, 255:256] + onehot[:, b * 256 + 255 : b * 256 + 256]
    rank = jnp.concatenate(ranks, axis=1).astype(jnp.int32)
    slot = ids * CAP + rank

    def pack(t):
        i = t * CHUNK + lax.broadcasted_iota(jnp.int32, (CHUNK, 128), 0)
        wanted = cluster_vec(me, i // CAP) * CAP + i % CAP
        pick = jnp.where(slot == wanted[:, 0:1], 1.0, 0.0)
        held = jnp.sum(pick, axis=1, keepdims=True)
        packed = jnp.dot(pick.astype(jnp.bfloat16), unit[...], preferred_element_type=jnp.float32)
        lane = lax.broadcasted_iota(jnp.int32, (CHUNK, 128), 1)
        first = packed[:, :128] + jnp.where(lane == 0, EMPTY * (1.0 - held), 0.0)
        return jnp.concatenate([first, packed[:, 128:]], axis=1).astype(jnp.bfloat16)

    def cluster_vec(me, k):
        return cluster_of(*target(me, k))

    def start(k, t):
        rows = pl.ds(pl.multiple_of(k * CAP, CAP), CAP)
        pltpu.make_async_remote_copy(
            src_ref=send.at[rows],
            dst_ref=recv.at[rows],
            send_sem=send_sem,
            recv_sem=recv_sem.at[t],
            device_id=device_id(*target(me, k)),
            device_id_type=MESH,
        ).start()

    for t in range(CHUNKS):
        chunk = pack(t)
        send[pl.ds(t * CHUNK, CHUNK), :] = chunk
        if t == 0:
            recv[pl.ds(0, CAP), :] = chunk[:CAP]
            pl.semaphore_wait(barrier, DEVICES - 1)
        lo = t * PER_CHUNK

        def go(k, _, t=t):
            start(k, t)
            return 0

        lax.fori_loop(max(lo, 1), lo + PER_CHUNK, go, 0)

    acc[...] = jnp.zeros_like(acc)

    def block(u, t, diagonal):
        keys = pl.ds(pl.multiple_of(u * CHUNK, CHUNK), CHUNK)
        queries = pl.ds(pl.multiple_of(t * CHUNK, CHUNK), CHUNK)
        s = lax.dot_general(recv[keys, :], recv[queries, :], NT, preferred_element_type=jnp.float32)
        keep = flags[keys, :]
        w = jnp.exp2(s * SCALE) * jnp.concatenate([keep, keep], axis=1)
        if diagonal:
            own = lax.broadcasted_iota(jnp.int32, w.shape, 0)
            other = lax.broadcasted_iota(jnp.int32, w.shape, 1)
            w = jnp.where(own == other, 0.0, w)
        acc[:, queries] += jnp.sum(w.reshape(CHUNK // 8, 8, CHUNK), axis=0)

    for t in range(CHUNKS):
        skip = CAP if t == 0 else 0
        landed = recv.at[pl.ds(t * CHUNK + skip, CHUNK - skip)]
        pltpu.make_async_copy(landed, landed, recv_sem.at[t]).wait()
        rows = pl.ds(t * CHUNK, CHUNK)
        head = recv[rows, :128].astype(jnp.float32)[:, 0:1]
        flags[rows, :] = jnp.broadcast_to(jnp.where(head < 1.125, 1.0, 0.0), (CHUNK, 128))
        block(t, t, True)

        def others(u, _, t=t):
            block(u, t, False)
            block(t, u, False)
            return 0

        if t:
            lax.fori_loop(0, t, others, 0)

    density = jnp.log(1.0 + jnp.sum(acc[...], axis=0, keepdims=True))

    i = lax.broadcasted_iota(jnp.int32, (DEVICES, SLOTS), 1) // CAP
    a, b, d, f = offset_of(i)
    sx, sy, sz, sc = (x - a + 4) % 4, (y - b + 4) % 4, (z - d + 4) % 4, (c + f) % 2
    source = (sx * 4 + sz) * 8 + sy * 2 + sc
    mine = lax.broadcasted_iota(jnp.int32, (DEVICES, SLOTS), 0) == source
    spread = jnp.where(
        lax.broadcasted_iota(jnp.int32, (SLOTS, 128), 0) % CAP
        == lax.broadcasted_iota(jnp.int32, (SLOTS, 128), 1),
        1.0, 0.0,
    ).astype(jnp.bfloat16)
    total = jnp.zeros((DEVICES, 128), jnp.float32)
    for part in split3(density):
        rows = jnp.where(mine, part.astype(jnp.float32), 0.0).astype(jnp.bfloat16)
        total = total + jnp.dot(rows, spread, preferred_element_type=jnp.float32)
    ret0[...] = total

    xz = x * 4 + z

    def stage1(j, _):
        to = (xz + j) % 16
        pltpu.make_async_remote_copy(
            src_ref=ret0.at[pl.ds(pl.multiple_of(to * 8, 8), 8)],
            dst_ref=ret1.at[pl.ds(pl.multiple_of(xz * 8, 8), 8)],
            send_sem=s1_sem,
            recv_sem=r1_sem,
            device_id=(to * 2 + c, y),
            device_id_type=MESH,
        ).start()
        return 0

    lax.fori_loop(1, 16, stage1, 0)
    own = pl.ds(pl.multiple_of(xz * 8, 8), 8)
    ret1[own, :] = ret0[own, :]
    came = ret1.at[pl.ds(0, 120)]
    pltpu.make_async_copy(came, came, r1_sem).wait()
    for j in range(8):
        ret2[pl.ds(j * 16, 16), :] = ret1[pl.ds(j, 16, stride=8), :]
    yc = y * 2 + c

    def stage2(j, _):
        to = (yc + j) % 8
        pltpu.make_async_remote_copy(
            src_ref=ret2.at[pl.ds(pl.multiple_of(to * 16, 16), 16)],
            dst_ref=ret3.at[pl.ds(pl.multiple_of(yc * 16, 16), 16)],
            send_sem=s2_sem,
            recv_sem=r2_sem,
            device_id=(xz * 2 + to % 2, to // 2),
            device_id_type=MESH,
        ).start()
        return 0

    lax.fori_loop(1, 8, stage2, 0)
    own = pl.ds(pl.multiple_of(yc * 16, 16), 16)
    ret3[own, :] = ret2[own, :]
    came = ret3.at[pl.ds(0, 112)]
    pltpu.make_async_copy(came, came, r2_sem).wait()

    back = jnp.transpose(ret3[...])[:CAP, :]
    found = jnp.zeros((CAP, ROWS), jnp.float32)
    for part in split3(back):
        found = found + jnp.dot(part, onehot16, preferred_element_type=jnp.float32)
    at = lax.broadcasted_iota(jnp.int32, (CAP, ROWS), 0) == rank
    out_ref[...] = jnp.sum(jnp.where(at, found, 0.0), axis=0, keepdims=True)

    gone = send.at[pl.ds(CAP, SLOTS - CAP)]
    pltpu.make_async_copy(gone, gone, send_sem).wait()
    gone = ret0.at[pl.ds(0, 120)]
    pltpu.make_async_copy(gone, gone, s1_sem).wait()
    gone = ret2.at[pl.ds(0, 112)]
    pltpu.make_async_copy(gone, gone, s2_sem).wait()


def shards(embeddings, cluster_ids):
    vmem = pl.BlockSpec(memory_space=pltpu.VMEM)
    density = pl.pallas_call(
        kernel,
        out_shape=jax.ShapeDtypeStruct((1, ROWS), jnp.float32),
        in_specs=[vmem, vmem],
        out_specs=vmem,
        scratch_shapes=[
            pltpu.VMEM((ROWS, WIDTH), jnp.bfloat16),
            pltpu.VMEM((SLOTS, WIDTH), jnp.bfloat16),
            pltpu.VMEM((SLOTS, WIDTH), jnp.bfloat16),
            pltpu.VMEM((SLOTS, 128), jnp.float32),
            pltpu.VMEM((8, SLOTS), jnp.float32),
            pltpu.VMEM((DEVICES, 128), jnp.float32),
            pltpu.VMEM((DEVICES, 128), jnp.float32),
            pltpu.VMEM((DEVICES, 128), jnp.float32),
            pltpu.VMEM((DEVICES, 128), jnp.float32),
            pltpu.SemaphoreType.DMA,
            pltpu.SemaphoreType.DMA((CHUNKS,)),
            pltpu.SemaphoreType.DMA,
            pltpu.SemaphoreType.DMA,
            pltpu.SemaphoreType.DMA,
            pltpu.SemaphoreType.DMA,
        ],
        compiler_params=pltpu.CompilerParams(
            collective_id=0, has_side_effects=True, vmem_limit_bytes=48 << 20
        ),
        name="density",
    )(embeddings, cluster_ids.reshape(1, ROWS))
    return density.reshape(ROWS)


def solution(mesh):
    placed = (P(("pool", "blk"), None), P(("pool", "blk"), None))
    return jax.shard_map(
        shards, mesh=mesh, in_specs=placed, out_specs=P(("pool", "blk")), check_vma=False
    )
```

```python
import jax
import jax.numpy as jnp
from jax import lax
from jax.experimental import pallas as pl
from jax.experimental.pallas import tpu as pltpu
from jax.sharding import PartitionSpec as P

EPSILON = 1e-06
SCALE = 50.0 * 1.4426950408889634
MESH = pl.DeviceIdType.MESH
ROWS = 1024
WIDTH = 1024
CAP = 16
CHIPS = 64
SLOTS = 2 * CHIPS * CAP
CHUNK = 256
CHUNKS = SLOTS // CHUNK
EMPTY = 1.25
NT = (((1,), (1,)), ((), ()))


def opposite(o):
    return tuple(-v % 4 for v in o)


def hops(o):
    return sum(min(v, 4 - v) for v in o)


def far_first():
    every = [(a, b, d) for a in range(4) for b in range(4) for d in range(4)]
    every.sort(key=lambda o: (-hops(o), o))
    pairs, singles = [], []
    for o in every:
        for turn in (o, o[2:] + o[:2], o[1:] + o[:1]):
            both = [turn, opposite(turn)]
            if both[0] == both[1]:
                if turn not in singles:
                    singles.append(turn)
            elif both not in pairs and both[::-1] not in pairs:
                pairs.append(both)
    order = []
    for t in range(8):
        count = 2 if t in (0, 1, 5, 7) else 0
        for both in pairs[: 4 - count // 2]:
            order += both
        pairs = pairs[4 - count // 2 :]
        at = len(order) - 8 + count if t < 7 else len(order)
        order[at:at] = singles[:count]
        singles = singles[count:]
    return order


ORDER = far_first()
BACK = [ORDER.index(opposite(o)) for o in ORDER]
GROUPS = [(t * CHUNK, CHUNK) for t in range(CHUNKS - 1)] + [
    (SLOTS - CHUNK, CHUNK // 2),
    (SLOTS - CHUNK // 2, CHUNK // 2),
]


def slot_of(j, f):
    return (j // 8) * CHUNK + f * (CHUNK // 2) + (j % 8) * CAP


def row_of(j):
    return (j // 8) * 8 + -j % 8


def split3(v):
    hi = v.astype(jnp.bfloat16)
    rest = v - hi.astype(jnp.float32)
    mid = rest.astype(jnp.bfloat16)
    lo = (rest - mid.astype(jnp.float32)).astype(jnp.bfloat16)
    return hi, mid, lo


def kernel(
    emb_hbm, ids_hbm, out_ref,
    emb, ids_ref, unit, send, recv, flags, acc, acc_rows, ret, sib, both, back,
    load_sem, ids_sem, send_sem, recv_sem, sib_send, sib_recv, back_send, back_recv,
):
    pool = lax.axis_index("pool")
    y = lax.axis_index("blk")
    x, z, c = lax.div(pool, 8), lax.rem(lax.div(pool, 2), 4), lax.rem(pool, 2)

    loads = []
    ids_copy = pltpu.make_async_copy(ids_hbm, ids_ref, ids_sem)
    ids_copy.start()
    for b in range(4):
        rows = pl.ds(b * 256, 256)
        copy = pltpu.make_async_copy(emb_hbm.at[rows], emb.at[rows], load_sem.at[b])
        copy.start()
        loads.append(copy)

    xs = [lax.rem(x + a, 4) for a in range(4)]
    ys = [lax.rem(y + a, 4) for a in range(4)]
    zs = [lax.rem(z + a, 4) for a in range(4)]
    cs = [c, 1 - c]
    px = [v * 8 for v in xs]
    pzc = [[zs[d] * 2 + cs[f] for f in range(2)] for d in range(4)]

    def device(j, f):
        a, b, d = ORDER[j]
        return (px[a] + pzc[d][f], ys[b])

    def chip(j):
        a, b, d = ORDER[j]
        return xs[a] * 16 + ys[b] * 4 + zs[d]

    barrier = pltpu.get_barrier_semaphore()
    for j in range(CHIPS):
        for f in range(2):
            if j < CHIPS - 1 or f:
                pl.semaphore_signal(
                    barrier, inc=1, device_id=device(j, f), device_id_type=MESH
                )

    ids_copy.wait()
    ids = ids_ref[...]
    cluster = lax.broadcasted_iota(jnp.int32, (128, ROWS), 0)
    onehot = jnp.where(cluster == ids, 1.0, 0.0)
    onehot16 = onehot.astype(jnp.bfloat16)
    upper = jnp.where(
        lax.broadcasted_iota(jnp.int32, (256, 256), 0)
        < lax.broadcasted_iota(jnp.int32, (256, 256), 1),
        1.0, 0.0,
    ).astype(jnp.bfloat16)
    carry = jnp.zeros((128, 1), jnp.float32)
    ranks = []
    for b in range(4):
        cols = slice(b * 256, (b + 1) * 256)
        before = jnp.dot(onehot16[:, cols], upper, preferred_element_type=jnp.float32) + carry
        ranks.append(jnp.sum(before * onehot[:, cols], axis=0, keepdims=True))
        carry = before[:, 255:256] + onehot[:, b * 256 + 255 : b * 256 + 256]
    rank = jnp.concatenate(ranks, axis=1).astype(jnp.int32)
    slot = ids * CAP + rank - lax.broadcasted_iota(jnp.int32, (CAP, ROWS), 0)

    for b in range(4):
        loads[b].wait()
        rows = pl.ds(b * 256, 256)
        e = emb[rows, :]
        squares = jnp.sum(e * e, axis=1, keepdims=True)
        unit[rows, :] = (e * lax.rsqrt(squares + EPSILON)).astype(jnp.bfloat16)

    lane0 = lax.broadcasted_iota(jnp.int32, (CHUNK, 128), 1) == 0

    def pack(t):
        pick = jnp.concatenate(
            [
                jnp.where(slot == (chip(8 * t + j) * 2 + cs[f]) * CAP, 1.0, 0.0)
                for f in range(2)
                for j in range(8)
            ],
            axis=0,
        )
        held = jnp.sum(pick, axis=1, keepdims=True)
        packed = jnp.dot(pick.astype(jnp.bfloat16), unit[...], preferred_element_type=jnp.float32)
        first = packed[:, :128] + jnp.where(lane0, EMPTY * (1.0 - held), 0.0)
        return jnp.concatenate([first, packed[:, 128:]], axis=1).astype(jnp.bfloat16)

    def start(j, f):
        group = j // 8 + (f if j >= CHIPS - 8 else 0)
        pltpu.make_async_remote_copy(
            src_ref=send.at[pl.ds(slot_of(j, f), CAP)],
            dst_ref=recv.at[pl.ds(slot_of(BACK[j], f), CAP)],
            send_sem=send_sem,
            recv_sem=recv_sem.at[group],
            device_id=device(j, f),
            device_id_type=MESH,
        ).start()

    own = slot_of(CHIPS - 1, 0)
    for t in range(CHUNKS):
        chunk = pack(t)
        send[pl.ds(t * CHUNK, CHUNK), :] = chunk
        if t == 0:
            pl.semaphore_wait(barrier, 2 * CHIPS - 1)
        if t < CHUNKS - 1:
            for j in range(8 * t, 8 * t + 8):
                for f in range(2):
                    start(j, f)
        else:
            recv[pl.ds(own, CAP), :] = chunk[own - t * CHUNK : own - t * CHUNK + CAP]
            for f in range(2):
                for j in range(8 * t, 8 * t + 8):
                    if j < CHIPS - 1 or f:
                        start(j, f)

    acc[...] = jnp.zeros_like(acc)
    acc_rows[...] = jnp.zeros_like(acc_rows)
    pick0 = jnp.where(lax.broadcasted_iota(jnp.int32, (8, 128), 1) == 0, 1.0, 0.0).astype(jnp.bfloat16)

    for g, (q0, n) in enumerate(GROUPS):
        landed = recv.at[pl.ds(q0, n - CAP if q0 <= own < q0 + n else n)]
        pltpu.make_async_copy(landed, landed, recv_sem.at[g]).wait()
        head = recv[q0 : q0 + n, :128]
        mark = head.astype(jnp.float32)[:, 0:1]
        flags[q0 : q0 + n, :] = jnp.broadcast_to(jnp.where(mark < 1.125, 1.0, 0.0), (n, 128))
        marks = lax.dot_general(pick0, head, NT, preferred_element_type=jnp.float32)
        keep_q = jnp.where(marks[0:1, :] < 1.125, 1.0, 0.0)
        queries = recv[q0 : q0 + n, :]
        pieces = [(k, min(512, q0 - k)) for k in range(0, q0, 512)] + [(q0, n)]
        for k0, m in pieces:
            s = lax.dot_general(recv[k0 : k0 + m, :], queries, NT, preferred_element_type=jnp.float32)
            w = jnp.exp2(s * SCALE)
            if k0 == q0:
                w = jnp.where(
                    lax.broadcasted_iota(jnp.int32, (n, n), 0)
                    == lax.broadcasted_iota(jnp.int32, (n, n), 1),
                    0.0, w,
                )
            keep_k = flags[k0 : k0 + m, :]
            if n > 128:
                keep_k = jnp.concatenate([keep_k] * (n // 128), axis=1)
            acc[:, q0 : q0 + n] += jnp.sum((w * keep_k).reshape(m // 8, 8, n), axis=0)
            if k0 < q0:
                w = w * keep_q
                acc_rows[k0 : k0 + m, :] += sum(w[:, i : i + 128] for i in range(0, n, 128))

    rows = acc_rows[...]
    hi = rows.astype(jnp.bfloat16)
    mid = (rows - hi.astype(jnp.float32)).astype(jnp.bfloat16)
    turned = lax.dot_general(
        jnp.ones((8, 256), jnp.bfloat16), jnp.concatenate([hi, mid], axis=1), NT,
        preferred_element_type=jnp.float32,
    )
    density = jnp.log(1.0 + jnp.sum(acc[...], axis=0, keepdims=True) + turned[0:1, :])
    for i in range(2 * CHUNKS):
        tile = jnp.broadcast_to(density[:, i * 128 : i * 128 + 128], (8, 128))
        ret[i // 2, i % 2] = pltpu.roll(tile, 0, 1, stride=CAP, stride_axis=0)

    exchange = pltpu.make_async_remote_copy(
        src_ref=ret.at[:, 1],
        dst_ref=sib,
        send_sem=sib_send,
        recv_sem=sib_recv,
        device_id=(pool + 1 - 2 * c, y),
        device_id_type=MESH,
    )
    exchange.start()
    exchange.wait()
    low = lax.broadcasted_iota(jnp.int32, (8, 128), 1) < CAP
    for i in range(CHUNKS):
        mine, other = ret[i, 0], sib[i]
        first = jnp.where(c == 0, mine, other)
        second = jnp.where(c == 0, other, mine)
        both[pl.ds(i * 8, 8), :] = jnp.where(low, first, pltpu.roll(second, CAP, 1))
    back[pl.ds(CHIPS - 1, 1), :] = both[pl.ds(row_of(CHIPS - 1), 1), :]
    for j in range(CHIPS - 1):
        pltpu.make_async_remote_copy(
            src_ref=both.at[pl.ds(row_of(j), 1)],
            dst_ref=back.at[pl.ds(BACK[j], 1)],
            send_sem=back_send,
            recv_sem=back_recv,
            device_id=device(j, 0),
            device_id_type=MESH,
        ).start()

    row = lax.broadcasted_iota(jnp.int32, (CHIPS, 1), 0)
    chips = jnp.zeros((CHIPS, 1), jnp.int32)
    for j in range(CHIPS):
        chips = jnp.where(row == j, chip(j), chips)
    at_chip = jnp.where(lax.div(ids, 2) == chips, 1.0, 0.0).astype(jnp.bfloat16)
    at_lane = lax.broadcasted_iota(jnp.int32, (2 * CAP, ROWS), 0) == lax.rem(ids, 2) * CAP + rank

    came = back.at[pl.ds(0, CHIPS - 1)]
    pltpu.make_async_copy(came, came, back_recv).wait()
    turned = jnp.transpose(back[...])[: 2 * CAP, :]
    found = jnp.zeros((2 * CAP, ROWS), jnp.float32)
    for part in split3(turned):
        found = found + jnp.dot(part, at_chip, preferred_element_type=jnp.float32)
    out_ref[...] = jnp.sum(jnp.where(at_lane, found, 0.0), axis=0, keepdims=True)

    gone = send.at[pl.ds(CAP, SLOTS - CAP)]
    pltpu.make_async_copy(gone, gone, send_sem).wait()
    pltpu.make_async_copy(came, came, back_send).wait()


def shards(embeddings, cluster_ids):
    anywhere = pl.BlockSpec(memory_space=pl.ANY)
    density = pl.pallas_call(
        kernel,
        out_shape=jax.ShapeDtypeStruct((1, ROWS), jnp.float32),
        in_specs=[anywhere, anywhere],
        out_specs=pl.BlockSpec(memory_space=pltpu.VMEM),
        scratch_shapes=[
            pltpu.VMEM((ROWS, WIDTH), jnp.float32),
            pltpu.VMEM((1, ROWS), jnp.int32),
            pltpu.VMEM((ROWS, WIDTH), jnp.bfloat16),
            pltpu.VMEM((SLOTS, WIDTH), jnp.bfloat16),
            pltpu.VMEM((SLOTS, WIDTH), jnp.bfloat16),
            pltpu.VMEM((SLOTS, 128), jnp.float32),
            pltpu.VMEM((8, SLOTS), jnp.float32),
            pltpu.VMEM((SLOTS, 128), jnp.float32),
            pltpu.VMEM((CHUNKS, 2, 8, 128), jnp.float32),
            pltpu.VMEM((CHUNKS, 8, 128), jnp.float32),
            pltpu.VMEM((CHIPS, 128), jnp.float32),
            pltpu.VMEM((CHIPS, 128), jnp.float32),
            pltpu.SemaphoreType.DMA((4,)),
            pltpu.SemaphoreType.DMA,
            pltpu.SemaphoreType.DMA,
            pltpu.SemaphoreType.DMA((len(GROUPS),)),
            pltpu.SemaphoreType.DMA,
            pltpu.SemaphoreType.DMA,
            pltpu.SemaphoreType.DMA,
            pltpu.SemaphoreType.DMA,
        ],
        compiler_params=pltpu.CompilerParams(
            collective_id=0, has_side_effects=True, vmem_limit_bytes=60 << 20
        ),
        name="density",
    )(embeddings, cluster_ids.reshape(1, ROWS))
    return density.reshape(ROWS)


def solution(mesh):
    placed = (P(("pool", "blk"), None), P(("pool", "blk"), None))
    return jax.shard_map(
        shards, mesh=mesh, in_specs=placed, out_specs=P(("pool", "blk")), check_vma=False
    )
```

```python
import jax
import jax.numpy as jnp
from jax import lax
from jax.experimental import pallas as pl
from jax.experimental.pallas import tpu as pltpu
from jax.sharding import PartitionSpec as P

EPSILON = 1e-06
SCALE = 50.0 * 1.4426950408889634
MESH = pl.DeviceIdType.MESH
ROWS = 1024
WIDTH = 1024
CAP = 16
CHIPS = 64
SLOTS = 2 * CHIPS * CAP
CHUNK = 256
CHUNKS = SLOTS // CHUNK
EMPTY = 1.25
NT = (((1,), (1,)), ((), ()))


def opposite(o):
    return tuple(-v % 4 for v in o)


def hops(o):
    return sum(min(v, 4 - v) for v in o)


def far_first():
    every = [(a, b, d) for a in range(4) for b in range(4) for d in range(4)]
    every.sort(key=lambda o: (-hops(o), o))
    pairs, singles = [], []
    for o in every:
        for turn in (o, o[2:] + o[:2], o[1:] + o[:1]):
            both = [turn, opposite(turn)]
            if both[0] == both[1]:
                if turn not in singles:
                    singles.append(turn)
            elif both not in pairs and both[::-1] not in pairs:
                pairs.append(both)
    order = []
    for t in range(8):
        count = 2 if t in (0, 1, 5, 7) else 0
        for both in pairs[: 4 - count // 2]:
            order += both
        pairs = pairs[4 - count // 2 :]
        at = len(order) - 8 + count if t < 7 else len(order)
        order[at:at] = singles[:count]
        singles = singles[count:]
    return order


ORDER = far_first()
BACK = [ORDER.index(opposite(o)) for o in ORDER]
TILES = [t for g in range(8) for t in ((g, 0), ((g + 4) % 8, 1))]
GROUPS = [(t * CHUNK, CHUNK) for t in range(CHUNKS - 1)] + [
    (SLOTS - CHUNK, CHUNK // 2),
    (SLOTS - CHUNK // 2, CHUNK // 2),
]


def slot_of(j, f):
    return TILES.index((j // 8, f)) * 8 * CAP + (j % 8) * CAP


def row_of(j):
    return (j // 8) * 8 + -j % 8


def split3(v):
    hi = v.astype(jnp.bfloat16)
    rest = v - hi.astype(jnp.float32)
    mid = rest.astype(jnp.bfloat16)
    lo = (rest - mid.astype(jnp.float32)).astype(jnp.bfloat16)
    return hi, mid, lo


def kernel(
    emb_hbm, ids_hbm, out_ref,
    emb, ids_ref, unit, send, recv, flags, acc, acc_rows, ret, sib, both, back,
    load_sem, ids_sem, send_sem, recv_sem, sib_send, sib_recv, back_send, back_recv,
):
    pool = lax.axis_index("pool")
    y = lax.axis_index("blk")
    x, z, c = lax.div(pool, 8), lax.rem(lax.div(pool, 2), 4), lax.rem(pool, 2)

    loads = []
    ids_copy = pltpu.make_async_copy(ids_hbm, ids_ref, ids_sem)
    ids_copy.start()
    for b in range(4):
        rows = pl.ds(b * 256, 256)
        copy = pltpu.make_async_copy(emb_hbm.at[rows], emb.at[rows], load_sem.at[b])
        copy.start()
        loads.append(copy)

    xs = [lax.rem(x + a, 4) for a in range(4)]
    ys = [lax.rem(y + a, 4) for a in range(4)]
    zs = [lax.rem(z + a, 4) for a in range(4)]
    cs = [c, 1 - c]
    px = [v * 8 for v in xs]
    pzc = [[zs[d] * 2 + cs[f] for f in range(2)] for d in range(4)]

    def device(j, f):
        a, b, d = ORDER[j]
        return (px[a] + pzc[d][f], ys[b])

    def chip(j):
        a, b, d = ORDER[j]
        return xs[a] * 16 + ys[b] * 4 + zs[d]

    barrier = pltpu.get_barrier_semaphore()
    for j in range(CHIPS):
        for f in range(2):
            if j < CHIPS - 1 or f:
                pl.semaphore_signal(
                    barrier, inc=1, device_id=device(j, f), device_id_type=MESH
                )

    ids_copy.wait()
    ids = ids_ref[...]
    cluster = lax.broadcasted_iota(jnp.int32, (128, ROWS), 0)
    onehot = jnp.where(cluster == ids, 1.0, 0.0)
    onehot16 = onehot.astype(jnp.bfloat16)
    upper = jnp.where(
        lax.broadcasted_iota(jnp.int32, (256, 256), 0)
        < lax.broadcasted_iota(jnp.int32, (256, 256), 1),
        1.0, 0.0,
    ).astype(jnp.bfloat16)
    carry = jnp.zeros((128, 1), jnp.float32)
    ranks = []
    for b in range(4):
        cols = slice(b * 256, (b + 1) * 256)
        before = jnp.dot(onehot16[:, cols], upper, preferred_element_type=jnp.float32) + carry
        ranks.append(jnp.sum(before * onehot[:, cols], axis=0, keepdims=True))
        carry = before[:, 255:256] + onehot[:, b * 256 + 255 : b * 256 + 256]
    rank = jnp.concatenate(ranks, axis=1).astype(jnp.int32)
    slot = ids * CAP + rank - lax.broadcasted_iota(jnp.int32, (CAP, ROWS), 0)

    for b in range(4):
        loads[b].wait()
        rows = pl.ds(b * 256, 256)
        e = emb[rows, :]
        squares = jnp.sum(e * e, axis=1, keepdims=True)
        unit[rows, :] = (e * lax.rsqrt(squares + EPSILON)).astype(jnp.bfloat16)

    lane0 = lax.broadcasted_iota(jnp.int32, (CHUNK, 128), 1) == 0

    def pack(t):
        pick = jnp.concatenate(
            [
                jnp.where(slot == (chip(8 * g + j) * 2 + cs[f]) * CAP, 1.0, 0.0)
                for g, f in TILES[2 * t : 2 * t + 2]
                for j in range(8)
            ],
            axis=0,
        )
        held = jnp.sum(pick, axis=1, keepdims=True)
        packed = jnp.dot(pick.astype(jnp.bfloat16), unit[...], preferred_element_type=jnp.float32)
        first = packed[:, :128] + jnp.where(lane0, EMPTY * (1.0 - held), 0.0)
        return jnp.concatenate([first, packed[:, 128:]], axis=1).astype(jnp.bfloat16)

    own = slot_of(CHIPS - 1, 0)

    def start(j, f):
        at = slot_of(j, f)
        group = max(g for g, (q0, _) in enumerate(GROUPS) if q0 <= at)
        pltpu.make_async_remote_copy(
            src_ref=send.at[pl.ds(at, CAP)],
            dst_ref=recv.at[pl.ds(slot_of(BACK[j], f), CAP)],
            send_sem=send_sem,
            recv_sem=recv_sem.at[group],
            device_id=device(j, f),
            device_id_type=MESH,
        ).start()

    for t in range(CHUNKS):
        chunk = pack(t)
        send[pl.ds(t * CHUNK, CHUNK), :] = chunk
        if t == 0:
            pl.semaphore_wait(barrier, 2 * CHIPS - 1)
        if t == own // CHUNK:
            recv[pl.ds(own, CAP), :] = chunk[own - t * CHUNK : own - t * CHUNK + CAP]
        for i in range(8):
            for g, f in TILES[2 * t : 2 * t + 2]:
                if 8 * g + i < CHIPS - 1 or f:
                    start(8 * g + i, f)

    acc[...] = jnp.zeros_like(acc)
    acc_rows[...] = jnp.zeros_like(acc_rows)
    pick0 = jnp.where(lax.broadcasted_iota(jnp.int32, (8, 128), 1) == 0, 1.0, 0.0).astype(jnp.bfloat16)

    for g, (q0, n) in enumerate(GROUPS):
        landed = recv.at[pl.ds(q0, n - CAP if q0 <= own < q0 + n else n)]
        pltpu.make_async_copy(landed, landed, recv_sem.at[g]).wait()
        head = recv[q0 : q0 + n, :128]
        mark = head.astype(jnp.float32)[:, 0:1]
        flags[q0 : q0 + n, :] = jnp.broadcast_to(jnp.where(mark < 1.125, 1.0, 0.0), (n, 128))
        marks = lax.dot_general(pick0, head, NT, preferred_element_type=jnp.float32)
        keep_q = jnp.where(marks[0:1, :] < 1.125, 1.0, 0.0)
        queries = recv[q0 : q0 + n, :]
        pieces = [(k, min(512, q0 - k)) for k in range(0, q0, 512)] + [(q0, n)]
        for k0, m in pieces:
            s = lax.dot_general(recv[k0 : k0 + m, :], queries, NT, preferred_element_type=jnp.float32)
            w = jnp.exp2(s * SCALE)
            if k0 == q0:
                w = jnp.where(
                    lax.broadcasted_iota(jnp.int32, (n, n), 0)
                    == lax.broadcasted_iota(jnp.int32, (n, n), 1),
                    0.0, w,
                )
            keep_k = flags[k0 : k0 + m, :]
            if n > 128:
                keep_k = jnp.concatenate([keep_k] * (n // 128), axis=1)
            acc[:, q0 : q0 + n] += jnp.sum((w * keep_k).reshape(m // 8, 8, n), axis=0)
            if k0 < q0:
                w = w * keep_q
                acc_rows[k0 : k0 + m, :] += sum(w[:, i : i + 128] for i in range(0, n, 128))

    rows = acc_rows[...]
    hi = rows.astype(jnp.bfloat16)
    mid = (rows - hi.astype(jnp.float32)).astype(jnp.bfloat16)
    turned = lax.dot_general(
        jnp.ones((8, 256), jnp.bfloat16), jnp.concatenate([hi, mid], axis=1), NT,
        preferred_element_type=jnp.float32,
    )
    density = jnp.log(1.0 + jnp.sum(acc[...], axis=0, keepdims=True) + turned[0:1, :])
    for i in range(2 * CHUNKS):
        tile = jnp.broadcast_to(density[:, i * 128 : i * 128 + 128], (8, 128))
        g, f = TILES[i]
        ret[f, g] = pltpu.roll(tile, 0, 1, stride=CAP, stride_axis=0)

    exchange = pltpu.make_async_remote_copy(
        src_ref=ret.at[1],
        dst_ref=sib,
        send_sem=sib_send,
        recv_sem=sib_recv,
        device_id=(pool + 1 - 2 * c, y),
        device_id_type=MESH,
    )
    exchange.start()
    exchange.wait()
    low = lax.broadcasted_iota(jnp.int32, (8, 128), 1) < CAP
    for i in range(CHUNKS):
        mine, other = ret[0, i], sib[i]
        first = jnp.where(c == 0, mine, other)
        second = jnp.where(c == 0, other, mine)
        both[pl.ds(i * 8, 8), :] = jnp.where(low, first, pltpu.roll(second, CAP, 1))
    back[pl.ds(CHIPS - 1, 1), :] = both[pl.ds(row_of(CHIPS - 1), 1), :]
    for j in range(CHIPS - 1):
        pltpu.make_async_remote_copy(
            src_ref=both.at[pl.ds(row_of(j), 1)],
            dst_ref=back.at[pl.ds(BACK[j], 1)],
            send_sem=back_send,
            recv_sem=back_recv,
            device_id=device(j, 0),
            device_id_type=MESH,
        ).start()

    row = lax.broadcasted_iota(jnp.int32, (CHIPS, 1), 0)
    chips = jnp.zeros((CHIPS, 1), jnp.int32)
    for j in range(CHIPS):
        chips = jnp.where(row == j, chip(j), chips)
    at_chip = jnp.where(lax.div(ids, 2) == chips, 1.0, 0.0).astype(jnp.bfloat16)
    at_lane = lax.broadcasted_iota(jnp.int32, (2 * CAP, ROWS), 0) == lax.rem(ids, 2) * CAP + rank

    came = back.at[pl.ds(0, CHIPS - 1)]
    pltpu.make_async_copy(came, came, back_recv).wait()
    turned = jnp.transpose(back[...])[: 2 * CAP, :]
    found = jnp.zeros((2 * CAP, ROWS), jnp.float32)
    for part in split3(turned):
        found = found + jnp.dot(part, at_chip, preferred_element_type=jnp.float32)
    out_ref[...] = jnp.sum(jnp.where(at_lane, found, 0.0), axis=0, keepdims=True)

    gone = send.at[pl.ds(CAP, SLOTS - CAP)]
    pltpu.make_async_copy(gone, gone, send_sem).wait()
    pltpu.make_async_copy(came, came, back_send).wait()


def shards(embeddings, cluster_ids):
    anywhere = pl.BlockSpec(memory_space=pltpu.HBM)
    density = pl.pallas_call(
        kernel,
        out_shape=jax.ShapeDtypeStruct((1, ROWS), jnp.float32),
        in_specs=[anywhere, anywhere],
        out_specs=pl.BlockSpec(memory_space=pltpu.VMEM),
        scratch_shapes=[
            pltpu.VMEM((ROWS, WIDTH), jnp.float32),
            pltpu.VMEM((1, ROWS), jnp.int32),
            pltpu.VMEM((ROWS, WIDTH), jnp.bfloat16),
            pltpu.VMEM((SLOTS, WIDTH), jnp.bfloat16),
            pltpu.VMEM((SLOTS, WIDTH), jnp.bfloat16),
            pltpu.VMEM((SLOTS, 128), jnp.float32),
            pltpu.VMEM((8, SLOTS), jnp.float32),
            pltpu.VMEM((SLOTS, 128), jnp.float32),
            pltpu.VMEM((2, CHUNKS, 8, 128), jnp.float32),
            pltpu.VMEM((CHUNKS, 8, 128), jnp.float32),
            pltpu.VMEM((CHIPS, 128), jnp.float32),
            pltpu.VMEM((CHIPS, 128), jnp.float32),
            pltpu.SemaphoreType.DMA((4,)),
            pltpu.SemaphoreType.DMA,
            pltpu.SemaphoreType.DMA,
            pltpu.SemaphoreType.DMA((len(GROUPS),)),
            pltpu.SemaphoreType.DMA,
            pltpu.SemaphoreType.DMA,
            pltpu.SemaphoreType.DMA,
            pltpu.SemaphoreType.DMA,
        ],
        compiler_params=pltpu.CompilerParams(
            collective_id=0, has_side_effects=True, vmem_limit_bytes=56 << 20
        ),
        name="density",
    )(embeddings, cluster_ids.reshape(1, ROWS))
    return density.reshape(ROWS)


def solution(mesh):
    placed = (P(("pool", "blk"), None), P(("pool", "blk"), None))
    return jax.shard_map(
        shards, mesh=mesh, in_specs=placed, out_specs=P(("pool", "blk")), check_vma=False
    )
```

```python
import jax
import jax.numpy as jnp
from jax import lax
from jax.experimental import pallas as pl
from jax.experimental.pallas import tpu as pltpu
from jax.sharding import PartitionSpec as P

EPSILON = 1e-06
SCALE = 50.0 * 1.4426950408889634
MESH = pl.DeviceIdType.MESH
ROWS = 1024
WIDTH = 1024
CAP = 16
CHIPS = 64
SLOTS = 2 * CHIPS * CAP
CHUNK = 256
CHUNKS = SLOTS // CHUNK
EMPTY = 1.25
NT = (((1,), (1,)), ((), ()))


def opposite(o):
    return tuple(-v % 4 for v in o)


def hops(o):
    return sum(min(v, 4 - v) for v in o)


def far_first():
    every = [(a, b, d) for a in range(4) for b in range(4) for d in range(4)]
    every.sort(key=lambda o: (-hops(o), o))
    pairs, singles = [], []
    for o in every:
        for turn in (o, o[2:] + o[:2], o[1:] + o[:1]):
            both = [turn, opposite(turn)]
            if both[0] == both[1]:
                if turn not in singles:
                    singles.append(turn)
            elif both not in pairs and both[::-1] not in pairs:
                pairs.append(both)
    order = []
    for t in range(8):
        count = 2 if t in (0, 1, 5, 7) else 0
        for both in pairs[: 4 - count // 2]:
            order += both
        pairs = pairs[4 - count // 2 :]
        at = len(order) - 8 + count if t < 7 else len(order)
        order[at:at] = singles[:count]
        singles = singles[count:]
    return order


ORDER = far_first()
BACK = [ORDER.index(opposite(o)) for o in ORDER]
TILES = [t for g in range(8) for t in (((g + 4) % 8, 1), (g, 0))]
GROUPS = [(t * CHUNK, CHUNK) for t in range(CHUNKS)]


def slot_of(j, f):
    return TILES.index((j // 8, f)) * 8 * CAP + (j % 8) * CAP


def row_of(j):
    return (j // 8) * 8 + -j % 8


def split3(v):
    hi = v.astype(jnp.bfloat16)
    rest = v - hi.astype(jnp.float32)
    mid = rest.astype(jnp.bfloat16)
    lo = (rest - mid.astype(jnp.float32)).astype(jnp.bfloat16)
    return hi, mid, lo


def kernel(
    emb_hbm, ids_hbm, out_ref,
    emb, ids_ref, unit, send, recv, flags, acc, acc_rows, ret, sib, both, back,
    load_sem, ids_sem, send_sem, recv_sem, sib_send, sib_recv, back_send, back_recv,
):
    pool = lax.axis_index("pool")
    y = lax.axis_index("blk")
    x, z, c = lax.div(pool, 8), lax.rem(lax.div(pool, 2), 4), lax.rem(pool, 2)

    loads = []
    ids_copy = pltpu.make_async_copy(ids_hbm, ids_ref, ids_sem)
    ids_copy.start()
    for b in range(4):
        rows = pl.ds(b * 256, 256)
        copy = pltpu.make_async_copy(emb_hbm.at[rows], emb.at[rows], load_sem.at[b])
        copy.start()
        loads.append(copy)

    xs = [lax.rem(x + a, 4) for a in range(4)]
    ys = [lax.rem(y + a, 4) for a in range(4)]
    zs = [lax.rem(z + a, 4) for a in range(4)]
    cs = [c, 1 - c]
    px = [v * 8 for v in xs]
    pzc = [[zs[d] * 2 + cs[f] for f in range(2)] for d in range(4)]

    def device(j, f):
        a, b, d = ORDER[j]
        return (px[a] + pzc[d][f], ys[b])

    def chip(j):
        a, b, d = ORDER[j]
        return xs[a] * 16 + ys[b] * 4 + zs[d]

    barrier = pltpu.get_barrier_semaphore()
    for j in range(CHIPS):
        for f in range(2):
            if j < CHIPS - 1 or f:
                pl.semaphore_signal(
                    barrier, inc=1, device_id=device(j, f), device_id_type=MESH
                )

    ids_copy.wait()
    ids = ids_ref[...]
    cluster = lax.broadcasted_iota(jnp.int32, (128, ROWS), 0)
    onehot = jnp.where(cluster == ids, 1.0, 0.0)
    onehot16 = onehot.astype(jnp.bfloat16)
    upper = jnp.where(
        lax.broadcasted_iota(jnp.int32, (256, 256), 0)
        < lax.broadcasted_iota(jnp.int32, (256, 256), 1),
        1.0, 0.0,
    ).astype(jnp.bfloat16)
    carry = jnp.zeros((128, 1), jnp.float32)
    ranks = []
    for b in range(4):
        cols = slice(b * 256, (b + 1) * 256)
        before = jnp.dot(onehot16[:, cols], upper, preferred_element_type=jnp.float32) + carry
        ranks.append(jnp.sum(before * onehot[:, cols], axis=0, keepdims=True))
        carry = before[:, 255:256] + onehot[:, b * 256 + 255 : b * 256 + 256]
    rank = jnp.concatenate(ranks, axis=1).astype(jnp.int32)
    slot = ids * CAP + rank - lax.broadcasted_iota(jnp.int32, (CAP, ROWS), 0)

    for b in range(4):
        loads[b].wait()
        rows = pl.ds(b * 256, 256)
        e = emb[rows, :]
        squares = jnp.sum(e * e, axis=1, keepdims=True)
        unit[rows, :] = (e * lax.rsqrt(squares + EPSILON)).astype(jnp.bfloat16)

    lane0 = lax.broadcasted_iota(jnp.int32, (CHUNK, 128), 1) == 0

    def pack(t):
        pick = jnp.concatenate(
            [
                jnp.where(slot == (chip(8 * g + j) * 2 + cs[f]) * CAP, 1.0, 0.0)
                for g, f in TILES[2 * t : 2 * t + 2]
                for j in range(8)
            ],
            axis=0,
        )
        held = jnp.sum(pick, axis=1, keepdims=True)
        packed = jnp.dot(pick.astype(jnp.bfloat16), unit[...], preferred_element_type=jnp.float32)
        first = packed[:, :128] + jnp.where(lane0, EMPTY * (1.0 - held), 0.0)
        return jnp.concatenate([first, packed[:, 128:]], axis=1).astype(jnp.bfloat16)

    own = slot_of(CHIPS - 1, 0)

    def start(j, f):
        at = slot_of(j, f)
        group = max(g for g, (q0, _) in enumerate(GROUPS) if q0 <= at)
        pltpu.make_async_remote_copy(
            src_ref=send.at[pl.ds(at, CAP)],
            dst_ref=recv.at[pl.ds(slot_of(BACK[j], f), CAP)],
            send_sem=send_sem,
            recv_sem=recv_sem.at[group],
            device_id=device(j, f),
            device_id_type=MESH,
        ).start()

    for t in range(CHUNKS):
        chunk = pack(t)
        send[pl.ds(t * CHUNK, CHUNK), :] = chunk
        if t == 0:
            pl.semaphore_wait(barrier, 2 * CHIPS - 1)
        if t == own // CHUNK:
            recv[pl.ds(own, CAP), :] = chunk[own - t * CHUNK : own - t * CHUNK + CAP]
        for i in range(8):
            for g, f in TILES[2 * t : 2 * t + 2][::-1]:
                if 8 * g + i < CHIPS - 1 or f:
                    start(8 * g + i, f)

    acc[...] = jnp.zeros_like(acc)
    acc_rows[...] = jnp.zeros_like(acc_rows)
    pick0 = jnp.where(lax.broadcasted_iota(jnp.int32, (8, 128), 1) == 0, 1.0, 0.0).astype(jnp.bfloat16)

    for g, (q0, n) in enumerate(GROUPS):
        landed = recv.at[pl.ds(q0, n - CAP if q0 <= own < q0 + n else n)]
        pltpu.make_async_copy(landed, landed, recv_sem.at[g]).wait()
        head = recv[q0 : q0 + n, :128]
        mark = head.astype(jnp.float32)[:, 0:1]
        flags[q0 : q0 + n, :] = jnp.broadcast_to(jnp.where(mark < 1.125, 1.0, 0.0), (n, 128))
        marks = lax.dot_general(pick0, head, NT, preferred_element_type=jnp.float32)
        keep_q = jnp.where(marks[0:1, :] < 1.125, 1.0, 0.0)
        queries = recv[q0 : q0 + n, :]
        pieces = [(k, min(512, q0 - k)) for k in range(0, q0, 512)] + [(q0, n)]
        for k0, m in pieces:
            s = lax.dot_general(recv[k0 : k0 + m, :], queries, NT, preferred_element_type=jnp.float32)
            w = jnp.exp2(s * SCALE)
            if k0 == q0:
                w = jnp.where(
                    lax.broadcasted_iota(jnp.int32, (n, n), 0)
                    == lax.broadcasted_iota(jnp.int32, (n, n), 1),
                    0.0, w,
                )
            keep_k = flags[k0 : k0 + m, :]
            if n > 128:
                keep_k = jnp.concatenate([keep_k] * (n // 128), axis=1)
            acc[:, q0 : q0 + n] += jnp.sum((w * keep_k).reshape(m // 8, 8, n), axis=0)
            if k0 < q0:
                w = w * keep_q
                acc_rows[k0 : k0 + m, :] += sum(w[:, i : i + 128] for i in range(0, n, 128))

    rows = acc_rows[...]
    hi = rows.astype(jnp.bfloat16)
    mid = (rows - hi.astype(jnp.float32)).astype(jnp.bfloat16)
    turned = lax.dot_general(
        jnp.ones((8, 256), jnp.bfloat16), jnp.concatenate([hi, mid], axis=1), NT,
        preferred_element_type=jnp.float32,
    )
    density = jnp.log(1.0 + jnp.sum(acc[...], axis=0, keepdims=True) + turned[0:1, :])
    for i in range(2 * CHUNKS):
        tile = jnp.broadcast_to(density[:, i * 128 : i * 128 + 128], (8, 128))
        g, f = TILES[i]
        ret[f, g] = pltpu.roll(tile, 0, 1, stride=CAP, stride_axis=0)

    exchange = pltpu.make_async_remote_copy(
        src_ref=ret.at[1],
        dst_ref=sib,
        send_sem=sib_send,
        recv_sem=sib_recv,
        device_id=(pool + 1 - 2 * c, y),
        device_id_type=MESH,
    )
    exchange.start()
    exchange.wait()
    low = lax.broadcasted_iota(jnp.int32, (8, 128), 1) < CAP
    for i in range(CHUNKS):
        mine, other = ret[0, i], sib[i]
        first = jnp.where(c == 0, mine, other)
        second = jnp.where(c == 0, other, mine)
        both[pl.ds(i * 8, 8), :] = jnp.where(low, first, pltpu.roll(second, CAP, 1))
    back[pl.ds(CHIPS - 1, 1), :] = both[pl.ds(row_of(CHIPS - 1), 1), :]
    for j in range(CHIPS - 1):
        pltpu.make_async_remote_copy(
            src_ref=both.at[pl.ds(row_of(j), 1)],
            dst_ref=back.at[pl.ds(BACK[j], 1)],
            send_sem=back_send,
            recv_sem=back_recv,
            device_id=device(j, 0),
            device_id_type=MESH,
        ).start()

    row = lax.broadcasted_iota(jnp.int32, (CHIPS, 1), 0)
    chips = jnp.zeros((CHIPS, 1), jnp.int32)
    for j in range(CHIPS):
        chips = jnp.where(row == j, chip(j), chips)
    at_chip = jnp.where(lax.div(ids, 2) == chips, 1.0, 0.0).astype(jnp.bfloat16)
    at_lane = lax.broadcasted_iota(jnp.int32, (2 * CAP, ROWS), 0) == lax.rem(ids, 2) * CAP + rank

    came = back.at[pl.ds(0, CHIPS - 1)]
    pltpu.make_async_copy(came, came, back_recv).wait()
    turned = jnp.transpose(back[...])[: 2 * CAP, :]
    found = jnp.zeros((2 * CAP, ROWS), jnp.float32)
    for part in split3(turned):
        found = found + jnp.dot(part, at_chip, preferred_element_type=jnp.float32)
    out_ref[...] = jnp.sum(jnp.where(at_lane, found, 0.0), axis=0, keepdims=True)

    gone = send.at[pl.ds(CAP, SLOTS - CAP)]
    pltpu.make_async_copy(gone, gone, send_sem).wait()
    pltpu.make_async_copy(came, came, back_send).wait()


def shards(embeddings, cluster_ids):
    anywhere = pl.BlockSpec(memory_space=pltpu.HBM)
    density = pl.pallas_call(
        kernel,
        out_shape=jax.ShapeDtypeStruct((1, ROWS), jnp.float32),
        in_specs=[anywhere, anywhere],
        out_specs=pl.BlockSpec(memory_space=pltpu.VMEM),
        scratch_shapes=[
            pltpu.VMEM((ROWS, WIDTH), jnp.float32),
            pltpu.VMEM((1, ROWS), jnp.int32),
            pltpu.VMEM((ROWS, WIDTH), jnp.bfloat16),
            pltpu.VMEM((SLOTS, WIDTH), jnp.bfloat16),
            pltpu.VMEM((SLOTS, WIDTH), jnp.bfloat16),
            pltpu.VMEM((SLOTS, 128), jnp.float32),
            pltpu.VMEM((8, SLOTS), jnp.float32),
            pltpu.VMEM((SLOTS, 128), jnp.float32),
            pltpu.VMEM((2, CHUNKS, 8, 128), jnp.float32),
            pltpu.VMEM((CHUNKS, 8, 128), jnp.float32),
            pltpu.VMEM((CHIPS, 128), jnp.float32),
            pltpu.VMEM((CHIPS, 128), jnp.float32),
            pltpu.SemaphoreType.DMA((4,)),
            pltpu.SemaphoreType.DMA,
            pltpu.SemaphoreType.DMA,
            pltpu.SemaphoreType.DMA((len(GROUPS),)),
            pltpu.SemaphoreType.DMA,
            pltpu.SemaphoreType.DMA,
            pltpu.SemaphoreType.DMA,
            pltpu.SemaphoreType.DMA,
        ],
        compiler_params=pltpu.CompilerParams(
            collective_id=0, has_side_effects=True, vmem_limit_bytes=56 << 20
        ),
        name="density",
    )(embeddings, cluster_ids.reshape(1, ROWS))
    return density.reshape(ROWS)


def solution(mesh):
    placed = (P(("pool", "blk"), None), P(("pool", "blk"), None))
    return jax.shard_map(
        shards, mesh=mesh, in_specs=placed, out_specs=P(("pool", "blk")), check_vma=False
    )
```

```python
import jax
import jax.numpy as jnp
from jax import lax
from jax.experimental import pallas as pl
from jax.experimental.pallas import tpu as pltpu
from jax.sharding import PartitionSpec as P

EPSILON = 1e-06
SCALE = 50.0 * 1.4426950408889634
MESH = pl.DeviceIdType.MESH
ROWS = 1024
WIDTH = 1024
CAP = 16
CHIPS = 64
SLOTS = 2 * CHIPS * CAP
CHUNK = 256
CHUNKS = SLOTS // CHUNK
EMPTY = 1.25
NT = (((1,), (1,)), ((), ()))


def opposite(o):
    return tuple(-v % 4 for v in o)


def hops(o):
    return sum(min(v, 4 - v) for v in o)


def far_first():
    every = [(a, b, d) for a in range(4) for b in range(4) for d in range(4)]
    every.sort(key=lambda o: (-hops(o), o))
    pairs, singles = [], []
    for o in every:
        for turn in (o, o[2:] + o[:2], o[1:] + o[:1]):
            both = [turn, opposite(turn)]
            if both[0] == both[1]:
                if turn not in singles:
                    singles.append(turn)
            elif both not in pairs and both[::-1] not in pairs:
                pairs.append(both)
    order = []
    for t in range(8):
        count = 2 if t in (0, 1, 5, 7) else 0
        for both in pairs[: 4 - count // 2]:
            order += both
        pairs = pairs[4 - count // 2 :]
        at = len(order) - 8 + count if t < 7 else len(order)
        order[at:at] = singles[:count]
        singles = singles[count:]
    return order


ORDER = far_first()
BACK = [ORDER.index(opposite(o)) for o in ORDER]
TILES = [t for g in range(8) for t in (((g + 4) % 8, 1), (g, 0))]
GROUPS = [(t * CHUNK, CHUNK) for t in range(CHUNKS)]


def slot_of(j, f):
    return TILES.index((j // 8, f)) * 8 * CAP + (j % 8) * CAP


def row_of(j):
    return (j // 8) * 8 + -j % 8


def split3(v):
    hi = v.astype(jnp.bfloat16)
    rest = v - hi.astype(jnp.float32)
    mid = rest.astype(jnp.bfloat16)
    lo = (rest - mid.astype(jnp.float32)).astype(jnp.bfloat16)
    return hi, mid, lo


def kernel(
    emb_hbm, ids_hbm, out_ref,
    emb, ids_ref, unit, send, recv, flags, acc, acc_rows, ret, sib, both, back,
    load_sem, ids_sem, send_sem, recv_sem, sib_send, sib_recv, back_send, back_recv,
):
    pool = lax.axis_index("pool")
    y = lax.axis_index("blk")
    x, z, c = lax.div(pool, 8), lax.rem(lax.div(pool, 2), 4), lax.rem(pool, 2)

    loads = []
    ids_copy = pltpu.make_async_copy(ids_hbm, ids_ref, ids_sem)
    ids_copy.start()
    for b in range(4):
        rows = pl.ds(b * 256, 256)
        copy = pltpu.make_async_copy(emb_hbm.at[rows], emb.at[rows], load_sem.at[b])
        copy.start()
        loads.append(copy)

    xs = [lax.rem(x + a, 4) for a in range(4)]
    ys = [lax.rem(y + a, 4) for a in range(4)]
    zs = [lax.rem(z + a, 4) for a in range(4)]
    cs = [c, 1 - c]
    px = [v * 8 for v in xs]
    pzc = [[zs[d] * 2 + cs[f] for f in range(2)] for d in range(4)]

    def device(j, f):
        a, b, d = ORDER[j]
        return (px[a] + pzc[d][f], ys[b])

    def chip(j):
        a, b, d = ORDER[j]
        return xs[a] * 16 + ys[b] * 4 + zs[d]

    barrier = pltpu.get_barrier_semaphore()
    for j in range(CHIPS):
        for f in range(2):
            if j < CHIPS - 1 or f:
                pl.semaphore_signal(
                    barrier, inc=1, device_id=device(j, f), device_id_type=MESH
                )

    ids_copy.wait()
    ids = ids_ref[...]
    cluster = lax.broadcasted_iota(jnp.int32, (128, ROWS), 0)
    onehot = jnp.where(cluster == ids, 1.0, 0.0)
    onehot16 = onehot.astype(jnp.bfloat16)
    upper = jnp.where(
        lax.broadcasted_iota(jnp.int32, (256, 256), 0)
        < lax.broadcasted_iota(jnp.int32, (256, 256), 1),
        1.0, 0.0,
    ).astype(jnp.bfloat16)
    carry = jnp.zeros((128, 1), jnp.float32)
    ranks = []
    for b in range(4):
        cols = slice(b * 256, (b + 1) * 256)
        before = jnp.dot(onehot16[:, cols], upper, preferred_element_type=jnp.float32) + carry
        ranks.append(jnp.sum(before * onehot[:, cols], axis=0, keepdims=True))
        carry = before[:, 255:256] + onehot[:, b * 256 + 255 : b * 256 + 256]
    rank = jnp.concatenate(ranks, axis=1).astype(jnp.int32)
    slot = ids * CAP + rank - lax.broadcasted_iota(jnp.int32, (CAP, ROWS), 0)

    for b in range(4):
        loads[b].wait()
        rows = pl.ds(b * 256, 256)
        e = emb[rows, :]
        squares = jnp.sum(e * e, axis=1, keepdims=True)
        unit[rows, :] = (e * lax.rsqrt(squares + EPSILON)).astype(jnp.bfloat16)

    lane0 = lax.broadcasted_iota(jnp.int32, (CHUNK, 128), 1) == 0

    def pack(t):
        pick = jnp.concatenate(
            [
                jnp.where(slot == (chip(8 * g + j) * 2 + cs[f]) * CAP, 1.0, 0.0)
                for g, f in TILES[2 * t : 2 * t + 2]
                for j in range(8)
            ],
            axis=0,
        )
        held = jnp.sum(pick, axis=1, keepdims=True)
        packed = jnp.dot(pick.astype(jnp.bfloat16), unit[...], preferred_element_type=jnp.float32)
        first = packed[:, :128] + jnp.where(lane0, EMPTY * (1.0 - held), 0.0)
        return jnp.concatenate([first, packed[:, 128:]], axis=1).astype(jnp.bfloat16)

    own = slot_of(CHIPS - 1, 0)

    def start(j, f):
        at = slot_of(j, f)
        group = max(g for g, (q0, _) in enumerate(GROUPS) if q0 <= at)
        pltpu.make_async_remote_copy(
            src_ref=send.at[pl.ds(at, CAP)],
            dst_ref=recv.at[pl.ds(slot_of(BACK[j], f), CAP)],
            send_sem=send_sem,
            recv_sem=recv_sem.at[group],
            device_id=device(j, f),
            device_id_type=MESH,
        ).start()

    for t in range(CHUNKS):
        chunk = pack(t)
        send[pl.ds(t * CHUNK, CHUNK), :] = chunk
        if t == 0:
            pl.semaphore_wait(barrier, 2 * CHIPS - 1)
        if t == own // CHUNK:
            recv[pl.ds(own, CAP), :] = chunk[own - t * CHUNK : own - t * CHUNK + CAP]
        for i in range(8):
            for g, f in TILES[2 * t : 2 * t + 2][::-1]:
                if 8 * g + i < CHIPS - 1 or f:
                    start(8 * g + i, f)

    acc[...] = jnp.zeros_like(acc)
    acc_rows[...] = jnp.zeros_like(acc_rows)
    pick0 = jnp.where(lax.broadcasted_iota(jnp.int32, (8, 128), 1) == 0, 1.0, 0.0).astype(jnp.bfloat16)

    for g, (q0, n) in enumerate(GROUPS):
        landed = recv.at[pl.ds(q0, n - CAP if q0 <= own < q0 + n else n)]
        pltpu.make_async_copy(landed, landed, recv_sem.at[g]).wait()
        head = recv[q0 : q0 + n, :128]
        mark = head.astype(jnp.float32)[:, 0:1]
        flags[q0 : q0 + n, :] = jnp.broadcast_to(jnp.where(mark < 1.125, 1.0, 0.0), (n, 128))
        marks = lax.dot_general(pick0, head, NT, preferred_element_type=jnp.float32)
        keep_q = jnp.where(marks[0:1, :] < 1.125, 1.0, 0.0)
        queries = recv[q0 : q0 + n, :]
        pieces = [(k, min(512, q0 - k)) for k in range(0, q0, 512)] + [(q0, n)]
        for k0, m in pieces:
            s = lax.dot_general(recv[k0 : k0 + m, :], queries, NT, preferred_element_type=jnp.float32)
            w = jnp.exp2(s * SCALE)
            if k0 == q0:
                w = jnp.where(
                    lax.broadcasted_iota(jnp.int32, (n, n), 0)
                    == lax.broadcasted_iota(jnp.int32, (n, n), 1),
                    0.0, w,
                )
            keep_k = flags[k0 : k0 + m, :]
            if n > 128:
                keep_k = jnp.concatenate([keep_k] * (n // 128), axis=1)
            acc[:, q0 : q0 + n] += jnp.sum((w * keep_k).reshape(m // 8, 8, n), axis=0)
            if k0 < q0:
                w = w * keep_q
                acc_rows[k0 : k0 + m, :] += sum(w[:, i : i + 128] for i in range(0, n, 128))

    rows = acc_rows[...]
    hi = rows.astype(jnp.bfloat16)
    mid = (rows - hi.astype(jnp.float32)).astype(jnp.bfloat16)
    turned = lax.dot_general(
        jnp.ones((8, 256), jnp.bfloat16), jnp.concatenate([hi, mid], axis=1), NT,
        preferred_element_type=jnp.float32,
    )
    density = jnp.log(1.0 + jnp.sum(acc[...], axis=0, keepdims=True) + turned[0:1, :])
    for i in range(2 * CHUNKS):
        tile = jnp.broadcast_to(density[:, i * 128 : i * 128 + 128], (8, 128))
        g, f = TILES[i]
        ret[f, g] = pltpu.roll(tile, 0, 1, stride=CAP, stride_axis=0)

    exchange = pltpu.make_async_remote_copy(
        src_ref=ret.at[1],
        dst_ref=sib,
        send_sem=sib_send,
        recv_sem=sib_recv,
        device_id=(pool + 1 - 2 * c, y),
        device_id_type=MESH,
    )
    exchange.start()
    exchange.wait()
    low = lax.broadcasted_iota(jnp.int32, (8, 128), 1) < CAP
    for i in range(CHUNKS):
        mine, other = ret[0, i], sib[i]
        first = jnp.where(c == 0, mine, other)
        second = jnp.where(c == 0, other, mine)
        both[pl.ds(i * 8, 8), :] = jnp.where(low, first, pltpu.roll(second, CAP, 1))
    back[pl.ds(CHIPS - 1, 1), :] = both[pl.ds(row_of(CHIPS - 1), 1), :]
    for j in range(CHIPS - 1):
        pltpu.make_async_remote_copy(
            src_ref=both.at[pl.ds(row_of(j), 1)],
            dst_ref=back.at[pl.ds(BACK[j], 1)],
            send_sem=back_send,
            recv_sem=back_recv,
            device_id=device(j, 0),
            device_id_type=MESH,
        ).start()

    row = lax.broadcasted_iota(jnp.int32, (CHIPS, 1), 0)
    chips = jnp.zeros((CHIPS, 1), jnp.int32)
    for j in range(CHIPS):
        chips = jnp.where(row == j, chip(j), chips)
    at_chip = jnp.where(lax.div(ids, 2) == chips, 1.0, 0.0).astype(jnp.bfloat16)
    at_lane = lax.broadcasted_iota(jnp.int32, (2 * CAP, ROWS), 0) == lax.rem(ids, 2) * CAP + rank

    came = back.at[pl.ds(0, CHIPS - 1)]
    pltpu.make_async_copy(came, came, back_recv).wait()
    turned = jnp.transpose(back[...])[: 2 * CAP, :]
    found = jnp.zeros((2 * CAP, ROWS), jnp.float32)
    for part in split3(turned):
        found = found + jnp.dot(part, at_chip, preferred_element_type=jnp.float32)
    out_ref[...] = jnp.sum(jnp.where(at_lane, found, 0.0), axis=0, keepdims=True)

    gone = send.at[pl.ds(CAP, SLOTS - CAP)]
    pltpu.make_async_copy(gone, gone, send_sem).wait()
    pltpu.make_async_copy(came, came, back_send).wait()


def shards(embeddings, cluster_ids):
    anywhere = pl.BlockSpec(memory_space=pltpu.HBM)
    density = pl.pallas_call(
        kernel,
        out_shape=jax.ShapeDtypeStruct((1, ROWS), jnp.float32),
        in_specs=[anywhere, anywhere],
        out_specs=pl.BlockSpec(memory_space=pltpu.VMEM),
        scratch_shapes=[
            pltpu.VMEM((ROWS, WIDTH), jnp.float32),
            pltpu.VMEM((1, ROWS), jnp.int32),
            pltpu.VMEM((ROWS, WIDTH), jnp.bfloat16),
            pltpu.VMEM((SLOTS, WIDTH), jnp.bfloat16),
            pltpu.VMEM((SLOTS, WIDTH), jnp.bfloat16),
            pltpu.VMEM((SLOTS, 128), jnp.float32),
            pltpu.VMEM((8, SLOTS), jnp.float32),
            pltpu.VMEM((SLOTS, 128), jnp.float32),
            pltpu.VMEM((2, CHUNKS, 8, 128), jnp.float32),
            pltpu.VMEM((CHUNKS, 8, 128), jnp.float32),
            pltpu.VMEM((CHIPS, 128), jnp.float32),
            pltpu.VMEM((CHIPS, 128), jnp.float32),
            pltpu.SemaphoreType.DMA((4,)),
            pltpu.SemaphoreType.DMA,
            pltpu.SemaphoreType.DMA,
            pltpu.SemaphoreType.DMA((len(GROUPS),)),
            pltpu.SemaphoreType.DMA,
            pltpu.SemaphoreType.DMA,
            pltpu.SemaphoreType.DMA,
            pltpu.SemaphoreType.DMA,
        ],
        compiler_params=pltpu.CompilerParams(
            collective_id=0, has_side_effects=True, vmem_limit_bytes=55228 << 10
        ),
        name="density",
    )(embeddings, cluster_ids.reshape(1, ROWS))
    return density.reshape(ROWS)


def solution(mesh):
    placed = (P(("pool", "blk"), None), P(("pool", "blk"), None))
    return jax.shard_map(
        shards, mesh=mesh, in_specs=placed, out_specs=P(("pool", "blk")), check_vma=False
    )
```

```python
import jax
import jax.numpy as jnp
from jax import lax
from jax.experimental import pallas as pl
from jax.experimental.pallas import tpu as pltpu
from jax.sharding import PartitionSpec as P

EPSILON = 1e-06
SCALE = 50.0 * 1.4426950408889634
MESH = pl.DeviceIdType.MESH
ROWS = 1024
WIDTH = 1024
CAP = 16
CHIPS = 64
SLOTS = 2 * CHIPS * CAP
CHUNK = 256
CHUNKS = SLOTS // CHUNK
EMPTY = 1.25
NT = (((1,), (1,)), ((), ()))


def opposite(o):
    return tuple(-v % 4 for v in o)


def hops(o):
    return sum(min(v, 4 - v) for v in o)


def far_first():
    every = [(a, b, d) for a in range(4) for b in range(4) for d in range(4)]
    every.sort(key=lambda o: (-hops(o), o))
    pairs, singles = [], []
    for o in every:
        for turn in (o, o[2:] + o[:2], o[1:] + o[:1]):
            both = [turn, opposite(turn)]
            if both[0] == both[1]:
                if turn not in singles:
                    singles.append(turn)
            elif both not in pairs and both[::-1] not in pairs:
                pairs.append(both)
    order = []
    for t in range(8):
        count = 2 if t in (0, 1, 5, 7) else 0
        for both in pairs[: 4 - count // 2]:
            order += both
        pairs = pairs[4 - count // 2 :]
        at = len(order) - 8 + count if t < 7 else len(order)
        order[at:at] = singles[:count]
        singles = singles[count:]
    return order


ORDER = far_first()
BACK = [ORDER.index(opposite(o)) for o in ORDER]
OTHER = (4, 5, 6, 7, 0, 1, 2, 3)
TILES = [t for g in range(8) for t in ((OTHER[g], 1), (g, 0))]
GROUPS = [(t * CHUNK, CHUNK) for t in range(CHUNKS)]


def slot_of(j, f):
    return TILES.index((j // 8, f)) * 8 * CAP + (j % 8) * CAP


def row_of(j):
    return (j // 8) * 8 + -j % 8


def split3(v):
    hi = v.astype(jnp.bfloat16)
    rest = v - hi.astype(jnp.float32)
    mid = rest.astype(jnp.bfloat16)
    lo = (rest - mid.astype(jnp.float32)).astype(jnp.bfloat16)
    return hi, mid, lo


def kernel(
    emb_hbm, ids_hbm, out_ref,
    emb, ids_ref, unit, send, recv, flags, acc, acc_rows, ret, sib, both, back,
    load_sem, ids_sem, send_sem, recv_sem, sib_send, sib_recv, back_send, back_recv,
):
    pool = lax.axis_index("pool")
    y = lax.axis_index("blk")
    x, z, c = lax.div(pool, 8), lax.rem(lax.div(pool, 2), 4), lax.rem(pool, 2)

    loads = []
    ids_copy = pltpu.make_async_copy(ids_hbm, ids_ref, ids_sem)
    ids_copy.start()
    for b in range(4):
        rows = pl.ds(b * 256, 256)
        copy = pltpu.make_async_copy(emb_hbm.at[rows], emb.at[rows], load_sem.at[b])
        copy.start()
        loads.append(copy)

    xs = [lax.rem(x + a, 4) for a in range(4)]
    ys = [lax.rem(y + a, 4) for a in range(4)]
    zs = [lax.rem(z + a, 4) for a in range(4)]
    cs = [c, 1 - c]
    px = [v * 8 for v in xs]
    pzc = [[zs[d] * 2 + cs[f] for f in range(2)] for d in range(4)]

    def device(j, f):
        a, b, d = ORDER[j]
        return (px[a] + pzc[d][f], ys[b])

    def chip(j):
        a, b, d = ORDER[j]
        return xs[a] * 16 + ys[b] * 4 + zs[d]

    barrier = pltpu.get_barrier_semaphore()
    for j in range(CHIPS):
        for f in range(2):
            if j < CHIPS - 1 or f:
                pl.semaphore_signal(
                    barrier, inc=1, device_id=device(j, f), device_id_type=MESH
                )

    ids_copy.wait()
    ids = ids_ref[...]
    cluster = lax.broadcasted_iota(jnp.int32, (128, ROWS), 0)
    onehot = jnp.where(cluster == ids, 1.0, 0.0)
    onehot16 = onehot.astype(jnp.bfloat16)
    upper = jnp.where(
        lax.broadcasted_iota(jnp.int32, (256, 256), 0)
        < lax.broadcasted_iota(jnp.int32, (256, 256), 1),
        1.0, 0.0,
    ).astype(jnp.bfloat16)
    carry = jnp.zeros((128, 1), jnp.float32)
    ranks = []
    for b in range(4):
        cols = slice(b * 256, (b + 1) * 256)
        before = jnp.dot(onehot16[:, cols], upper, preferred_element_type=jnp.float32) + carry
        ranks.append(jnp.sum(before * onehot[:, cols], axis=0, keepdims=True))
        carry = before[:, 255:256] + onehot[:, b * 256 + 255 : b * 256 + 256]
    rank = jnp.concatenate(ranks, axis=1).astype(jnp.int32)
    slot = ids * CAP + rank - lax.broadcasted_iota(jnp.int32, (CAP, ROWS), 0)

    for b in range(4):
        loads[b].wait()
        rows = pl.ds(b * 256, 256)
        e = emb[rows, :]
        squares = jnp.sum(e * e, axis=1, keepdims=True)
        unit[rows, :] = (e * lax.rsqrt(squares + EPSILON)).astype(jnp.bfloat16)

    lane0 = lax.broadcasted_iota(jnp.int32, (CHUNK, 128), 1) == 0

    def pack(t):
        pick = jnp.concatenate(
            [
                jnp.where(slot == (chip(8 * g + j) * 2 + cs[f]) * CAP, 1.0, 0.0)
                for g, f in TILES[2 * t : 2 * t + 2]
                for j in range(8)
            ],
            axis=0,
        )
        held = jnp.sum(pick, axis=1, keepdims=True)
        packed = jnp.dot(pick.astype(jnp.bfloat16), unit[...], preferred_element_type=jnp.float32)
        first = packed[:, :128] + jnp.where(lane0, EMPTY * (1.0 - held), 0.0)
        return jnp.concatenate([first, packed[:, 128:]], axis=1).astype(jnp.bfloat16)

    own = slot_of(CHIPS - 1, 0)

    def start(j, f):
        at = slot_of(j, f)
        group = max(g for g, (q0, _) in enumerate(GROUPS) if q0 <= at)
        pltpu.make_async_remote_copy(
            src_ref=send.at[pl.ds(at, CAP)],
            dst_ref=recv.at[pl.ds(slot_of(BACK[j], f), CAP)],
            send_sem=send_sem,
            recv_sem=recv_sem.at[group],
            device_id=device(j, f),
            device_id_type=MESH,
        ).start()

    for t in range(CHUNKS):
        chunk = pack(t)
        send[pl.ds(t * CHUNK, CHUNK), :] = chunk
        if t == 0:
            pl.semaphore_wait(barrier, 2 * CHIPS - 1)
        if t == own // CHUNK:
            recv[pl.ds(own, CAP), :] = chunk[own - t * CHUNK : own - t * CHUNK + CAP]
        for i in range(8):
            for g, f in TILES[2 * t : 2 * t + 2][::-1]:
                j = 8 * g + (i + 4 * f) % 8
                if j < CHIPS - 1 or f:
                    start(j, f)

    acc[...] = jnp.zeros_like(acc)
    acc_rows[...] = jnp.zeros_like(acc_rows)
    pick0 = jnp.where(lax.broadcasted_iota(jnp.int32, (8, 128), 1) == 0, 1.0, 0.0).astype(jnp.bfloat16)

    for g, (q0, n) in enumerate(GROUPS):
        landed = recv.at[pl.ds(q0, n - CAP if q0 <= own < q0 + n else n)]
        pltpu.make_async_copy(landed, landed, recv_sem.at[g]).wait()
        head = recv[q0 : q0 + n, :128]
        mark = head.astype(jnp.float32)[:, 0:1]
        flags[q0 : q0 + n, :] = jnp.broadcast_to(jnp.where(mark < 1.125, 1.0, 0.0), (n, 128))
        marks = lax.dot_general(pick0, head, NT, preferred_element_type=jnp.float32)
        keep_q = jnp.where(marks[0:1, :] < 1.125, 1.0, 0.0)
        queries = recv[q0 : q0 + n, :]
        pieces = [(k, min(512, q0 - k)) for k in range(0, q0, 512)] + [(q0, n)]
        for k0, m in pieces:
            s = lax.dot_general(recv[k0 : k0 + m, :], queries, NT, preferred_element_type=jnp.float32)
            w = jnp.exp2(s * SCALE)
            if k0 == q0:
                w = jnp.where(
                    lax.broadcasted_iota(jnp.int32, (n, n), 0)
                    == lax.broadcasted_iota(jnp.int32, (n, n), 1),
                    0.0, w,
                )
            keep_k = flags[k0 : k0 + m, :]
            if n > 128:
                keep_k = jnp.concatenate([keep_k] * (n // 128), axis=1)
            acc[:, q0 : q0 + n] += jnp.sum((w * keep_k).reshape(m // 8, 8, n), axis=0)
            if k0 < q0:
                w = w * keep_q
                acc_rows[k0 : k0 + m, :] += sum(w[:, i : i + 128] for i in range(0, n, 128))

    rows = acc_rows[...]
    hi = rows.astype(jnp.bfloat16)
    mid = (rows - hi.astype(jnp.float32)).astype(jnp.bfloat16)
    turned = lax.dot_general(
        jnp.ones((8, 256), jnp.bfloat16), jnp.concatenate([hi, mid], axis=1), NT,
        preferred_element_type=jnp.float32,
    )
    density = jnp.log(1.0 + jnp.sum(acc[...], axis=0, keepdims=True) + turned[0:1, :])
    for i in range(2 * CHUNKS):
        tile = jnp.broadcast_to(density[:, i * 128 : i * 128 + 128], (8, 128))
        g, f = TILES[i]
        ret[f, g] = pltpu.roll(tile, 0, 1, stride=CAP, stride_axis=0)

    exchange = pltpu.make_async_remote_copy(
        src_ref=ret.at[1],
        dst_ref=sib,
        send_sem=sib_send,
        recv_sem=sib_recv,
        device_id=(pool + 1 - 2 * c, y),
        device_id_type=MESH,
    )
    exchange.start()
    exchange.wait()
    low = lax.broadcasted_iota(jnp.int32, (8, 128), 1) < CAP
    for i in range(CHUNKS):
        mine, other = ret[0, i], sib[i]
        first = jnp.where(c == 0, mine, other)
        second = jnp.where(c == 0, other, mine)
        both[pl.ds(i * 8, 8), :] = jnp.where(low, first, pltpu.roll(second, CAP, 1))
    back[pl.ds(CHIPS - 1, 1), :] = both[pl.ds(row_of(CHIPS - 1), 1), :]
    for j in range(CHIPS - 1):
        pltpu.make_async_remote_copy(
            src_ref=both.at[pl.ds(row_of(j), 1)],
            dst_ref=back.at[pl.ds(BACK[j], 1)],
            send_sem=back_send,
            recv_sem=back_recv,
            device_id=device(j, 0),
            device_id_type=MESH,
        ).start()

    row = lax.broadcasted_iota(jnp.int32, (CHIPS, 1), 0)
    chips = jnp.zeros((CHIPS, 1), jnp.int32)
    for j in range(CHIPS):
        chips = jnp.where(row == j, chip(j), chips)
    at_chip = jnp.where(lax.div(ids, 2) == chips, 1.0, 0.0).astype(jnp.bfloat16)
    at_lane = lax.broadcasted_iota(jnp.int32, (2 * CAP, ROWS), 0) == lax.rem(ids, 2) * CAP + rank

    came = back.at[pl.ds(0, CHIPS - 1)]
    pltpu.make_async_copy(came, came, back_recv).wait()
    turned = jnp.transpose(back[...])[: 2 * CAP, :]
    found = jnp.zeros((2 * CAP, ROWS), jnp.float32)
    for part in split3(turned):
        found = found + jnp.dot(part, at_chip, preferred_element_type=jnp.float32)
    out_ref[...] = jnp.sum(jnp.where(at_lane, found, 0.0), axis=0, keepdims=True)

    gone = send.at[pl.ds(CAP, SLOTS - CAP)]
    pltpu.make_async_copy(gone, gone, send_sem).wait()
    pltpu.make_async_copy(came, came, back_send).wait()


def shards(embeddings, cluster_ids):
    anywhere = pl.BlockSpec(memory_space=pltpu.HBM)
    density = pl.pallas_call(
        kernel,
        out_shape=jax.ShapeDtypeStruct((1, ROWS), jnp.float32),
        in_specs=[anywhere, anywhere],
        out_specs=pl.BlockSpec(memory_space=pltpu.VMEM),
        scratch_shapes=[
            pltpu.VMEM((ROWS, WIDTH), jnp.float32),
            pltpu.VMEM((1, ROWS), jnp.int32),
            pltpu.VMEM((ROWS, WIDTH), jnp.bfloat16),
            pltpu.VMEM((SLOTS, WIDTH), jnp.bfloat16),
            pltpu.VMEM((SLOTS, WIDTH), jnp.bfloat16),
            pltpu.VMEM((SLOTS, 128), jnp.float32),
            pltpu.VMEM((8, SLOTS), jnp.float32),
            pltpu.VMEM((SLOTS, 128), jnp.float32),
            pltpu.VMEM((2, CHUNKS, 8, 128), jnp.float32),
            pltpu.VMEM((CHUNKS, 8, 128), jnp.float32),
            pltpu.VMEM((CHIPS, 128), jnp.float32),
            pltpu.VMEM((CHIPS, 128), jnp.float32),
            pltpu.SemaphoreType.DMA((4,)),
            pltpu.SemaphoreType.DMA,
            pltpu.SemaphoreType.DMA,
            pltpu.SemaphoreType.DMA((len(GROUPS),)),
            pltpu.SemaphoreType.DMA,
            pltpu.SemaphoreType.DMA,
            pltpu.SemaphoreType.DMA,
            pltpu.SemaphoreType.DMA,
        ],
        compiler_params=pltpu.CompilerParams(
            collective_id=0, has_side_effects=True, vmem_limit_bytes=55228 << 10
        ),
        name="density",
    )(embeddings, cluster_ids.reshape(1, ROWS))
    return density.reshape(ROWS)


def solution(mesh):
    placed = (P(("pool", "blk"), None), P(("pool", "blk"), None))
    return jax.shard_map(
        shards, mesh=mesh, in_specs=placed, out_specs=P(("pool", "blk")), check_vma=False
    )
```

```python
import jax
import jax.numpy as jnp
from jax import lax
from jax.experimental import pallas as pl
from jax.experimental.pallas import tpu as pltpu
from jax.sharding import PartitionSpec as P

EPSILON = 1e-06
SCALE = 50.0 * 1.4426950408889634
MESH = pl.DeviceIdType.MESH
ROWS = 1024
WIDTH = 1024
CAP = 16
CHIPS = 64
SLOTS = 2 * CHIPS * CAP
CHUNK = 256
CHUNKS = SLOTS // CHUNK
EMPTY = 1.25
NT = (((1,), (1,)), ((), ()))


def opposite(o):
    return tuple(-v % 4 for v in o)


def hops(o):
    return sum(min(v, 4 - v) for v in o)


def far_first():
    every = [(a, b, d) for a in range(4) for b in range(4) for d in range(4)]
    every.sort(key=lambda o: (-hops(o), o))
    pairs, singles = [], []
    for o in every:
        for turn in (o, o[2:] + o[:2], o[1:] + o[:1]):
            both = [turn, opposite(turn)]
            if both[0] == both[1]:
                if turn not in singles:
                    singles.append(turn)
            elif both not in pairs and both[::-1] not in pairs:
                pairs.append(both)
    order = []
    for t in range(8):
        count = 2 if t in (0, 1, 5, 7) else 0
        for both in pairs[: 4 - count // 2]:
            order += both
        pairs = pairs[4 - count // 2 :]
        at = len(order) - 8 + count if t < 7 else len(order)
        order[at:at] = singles[:count]
        singles = singles[count:]
    return order


ORDER = far_first()
BACK = [ORDER.index(opposite(o)) for o in ORDER]
OTHER = (4, 5, 6, 7, 0, 1, 2, 3)
TILES = [t for g in range(8) for t in ((OTHER[g], 1), (g, 0))]
GROUPS = [(t * CHUNK, CHUNK) for t in range(CHUNKS)]


def slot_of(j, f):
    return TILES.index((j // 8, f)) * 8 * CAP + (j % 8) * CAP


def row_of(j):
    return (j // 8) * 8 + -j % 8


def split3(v):
    hi = v.astype(jnp.bfloat16)
    rest = v - hi.astype(jnp.float32)
    mid = rest.astype(jnp.bfloat16)
    lo = (rest - mid.astype(jnp.float32)).astype(jnp.bfloat16)
    return hi, mid, lo


def kernel(
    emb_hbm, ids_hbm, out_ref,
    emb, ids_ref, unit, send, recv, flags, acc, acc_rows, ret, sib, both, back,
    load_sem, ids_sem, send_sem, recv_sem, sib_send, sib_recv, back_send, back_recv,
):
    pool = lax.axis_index("pool")
    y = lax.axis_index("blk")
    x, z, c = lax.div(pool, 8), lax.rem(lax.div(pool, 2), 4), lax.rem(pool, 2)

    loads = []
    ids_copy = pltpu.make_async_copy(ids_hbm, ids_ref, ids_sem)
    ids_copy.start()
    for b in range(4):
        rows = pl.ds(b * 256, 256)
        copy = pltpu.make_async_copy(emb_hbm.at[rows], emb.at[rows], load_sem.at[b])
        copy.start()
        loads.append(copy)

    xs = [lax.rem(x + a, 4) for a in range(4)]
    ys = [lax.rem(y + a, 4) for a in range(4)]
    zs = [lax.rem(z + a, 4) for a in range(4)]
    cs = [c, 1 - c]
    px = [v * 8 for v in xs]
    pzc = [[zs[d] * 2 + cs[f] for f in range(2)] for d in range(4)]

    def device(j, f):
        a, b, d = ORDER[j]
        return (px[a] + pzc[d][f], ys[b])

    def chip(j):
        a, b, d = ORDER[j]
        return xs[a] * 16 + ys[b] * 4 + zs[d]

    barrier = pltpu.get_barrier_semaphore()
    for j in range(CHIPS):
        for f in range(2):
            if j < CHIPS - 1 or f:
                pl.semaphore_signal(
                    barrier, inc=1, device_id=device(j, f), device_id_type=MESH
                )

    ids_copy.wait()
    ids = ids_ref[...]
    cluster = lax.broadcasted_iota(jnp.int32, (128, ROWS), 0)
    onehot = jnp.where(cluster == ids, 1.0, 0.0)
    onehot16 = onehot.astype(jnp.bfloat16)
    upper = jnp.where(
        lax.broadcasted_iota(jnp.int32, (256, 256), 0)
        < lax.broadcasted_iota(jnp.int32, (256, 256), 1),
        1.0, 0.0,
    ).astype(jnp.bfloat16)
    carry = jnp.zeros((128, 1), jnp.float32)
    ranks = []
    for b in range(4):
        cols = slice(b * 256, (b + 1) * 256)
        before = jnp.dot(onehot16[:, cols], upper, preferred_element_type=jnp.float32) + carry
        ranks.append(jnp.sum(before * onehot[:, cols], axis=0, keepdims=True))
        carry = before[:, 255:256] + onehot[:, b * 256 + 255 : b * 256 + 256]
    rank = jnp.concatenate(ranks, axis=1).astype(jnp.int32)
    slot = ids * CAP + rank - lax.broadcasted_iota(jnp.int32, (CAP, ROWS), 0)

    for b in range(4):
        loads[b].wait()
        rows = pl.ds(b * 256, 256)
        e = emb[rows, :]
        squares = jnp.sum(e * e, axis=1, keepdims=True)
        unit[rows, :] = (e * lax.rsqrt(squares + EPSILON)).astype(jnp.bfloat16)

    lane0 = lax.broadcasted_iota(jnp.int32, (CHUNK, 128), 1) == 0

    def pack(t):
        pick = jnp.concatenate(
            [
                jnp.where(slot == (chip(8 * g + j) * 2 + cs[f]) * CAP, 1.0, 0.0)
                for g, f in TILES[2 * t : 2 * t + 2]
                for j in range(8)
            ],
            axis=0,
        )
        held = jnp.sum(pick, axis=1, keepdims=True)
        packed = jnp.dot(pick.astype(jnp.bfloat16), unit[...], preferred_element_type=jnp.float32)
        first = packed[:, :128] + jnp.where(lane0, EMPTY * (1.0 - held), 0.0)
        return jnp.concatenate([first, packed[:, 128:]], axis=1).astype(jnp.bfloat16)

    own = slot_of(CHIPS - 1, 0)

    def start(j, f):
        at = slot_of(j, f)
        group = max(g for g, (q0, _) in enumerate(GROUPS) if q0 <= at)
        pltpu.make_async_remote_copy(
            src_ref=send.at[pl.ds(at, CAP)],
            dst_ref=recv.at[pl.ds(slot_of(BACK[j], f), CAP)],
            send_sem=send_sem,
            recv_sem=recv_sem.at[group],
            device_id=device(j, f),
            device_id_type=MESH,
        ).start()

    for t in range(CHUNKS):
        chunk = pack(t)
        send[pl.ds(t * CHUNK, CHUNK), :] = chunk
        if t == 0:
            pl.semaphore_wait(barrier, 2 * CHIPS - 1)
        if t == own // CHUNK:
            recv[pl.ds(own, CAP), :] = chunk[own - t * CHUNK : own - t * CHUNK + CAP]
        for i in range(8):
            for g, f in TILES[2 * t : 2 * t + 2][::-1]:
                j = 8 * g + (i + 4 * f) % 8
                if j < CHIPS - 1 or f:
                    start(j, f)

    acc[...] = jnp.zeros_like(acc)
    acc_rows[...] = jnp.zeros_like(acc_rows)
    pick0 = jnp.where(lax.broadcasted_iota(jnp.int32, (8, 128), 1) == 0, 1.0, 0.0).astype(jnp.bfloat16)

    for g, (q0, n) in enumerate(GROUPS):
        landed = recv.at[pl.ds(q0, n - CAP if q0 <= own < q0 + n else n)]
        pltpu.make_async_copy(landed, landed, recv_sem.at[g]).wait()
        head = recv[q0 : q0 + n, :128]
        mark = head.astype(jnp.float32)[:, 0:1]
        flags[q0 : q0 + n, :] = jnp.broadcast_to(jnp.where(mark < 1.125, 1.0, 0.0), (n, 128))
        marks = lax.dot_general(pick0, head, NT, preferred_element_type=jnp.float32)
        keep_q = jnp.where(marks[0:1, :] < 1.125, 1.0, 0.0)
        queries = recv[q0 : q0 + n, :]
        pieces = [(k, min(512, q0 - k)) for k in range(0, q0, 512)] + [(q0, n)]
        for k0, m in pieces:
            s = lax.dot_general(recv[k0 : k0 + m, :], queries, NT, preferred_element_type=jnp.float32)
            w = jnp.exp2(s * SCALE)
            if k0 == q0:
                w = jnp.where(
                    lax.broadcasted_iota(jnp.int32, (n, n), 0)
                    == lax.broadcasted_iota(jnp.int32, (n, n), 1),
                    0.0, w,
                )
            keep_k = flags[k0 : k0 + m, :]
            if n > 128:
                keep_k = jnp.concatenate([keep_k] * (n // 128), axis=1)
            acc[:, q0 : q0 + n] += jnp.sum((w * keep_k).reshape(m // 8, 8, n), axis=0)
            if k0 < q0:
                w = w * keep_q
                acc_rows[k0 : k0 + m, :] += sum(w[:, i : i + 128] for i in range(0, n, 128))

    rows = acc_rows[...]
    hi = rows.astype(jnp.bfloat16)
    mid = (rows - hi.astype(jnp.float32)).astype(jnp.bfloat16)
    turned = lax.dot_general(
        jnp.ones((8, 256), jnp.bfloat16), jnp.concatenate([hi, mid], axis=1), NT,
        preferred_element_type=jnp.float32,
    )
    density = jnp.log(1.0 + jnp.sum(acc[...], axis=0, keepdims=True) + turned[0:1, :])
    for i in range(2 * CHUNKS):
        tile = jnp.broadcast_to(density[:, i * 128 : i * 128 + 128], (8, 128))
        g, f = TILES[i]
        ret[f, g] = pltpu.roll(tile, 0, 1, stride=CAP, stride_axis=0)

    exchange = pltpu.make_async_remote_copy(
        src_ref=ret.at[1],
        dst_ref=sib,
        send_sem=sib_send,
        recv_sem=sib_recv,
        device_id=(pool + 1 - 2 * c, y),
        device_id_type=MESH,
    )
    exchange.start()
    exchange.wait()
    low = lax.broadcasted_iota(jnp.int32, (8, 128), 1) < CAP
    for i in range(CHUNKS):
        mine, other = ret[0, i], sib[i]
        first = jnp.where(c == 0, mine, other)
        second = jnp.where(c == 0, other, mine)
        both[pl.ds(i * 8, 8), :] = jnp.where(low, first, pltpu.roll(second, CAP, 1))
    back[pl.ds(CHIPS - 1, 1), :] = both[pl.ds(row_of(CHIPS - 1), 1), :]
    for j in sorted(range(CHIPS - 1), key=lambda j: -hops(ORDER[j])):
        pltpu.make_async_remote_copy(
            src_ref=both.at[pl.ds(row_of(j), 1)],
            dst_ref=back.at[pl.ds(BACK[j], 1)],
            send_sem=back_send,
            recv_sem=back_recv,
            device_id=device(j, 0),
            device_id_type=MESH,
        ).start()

    row = lax.broadcasted_iota(jnp.int32, (CHIPS, 1), 0)
    chips = jnp.zeros((CHIPS, 1), jnp.int32)
    for j in range(CHIPS):
        chips = jnp.where(row == j, chip(j), chips)
    at_chip = jnp.where(lax.div(ids, 2) == chips, 1.0, 0.0).astype(jnp.bfloat16)
    at_lane = lax.broadcasted_iota(jnp.int32, (2 * CAP, ROWS), 0) == lax.rem(ids, 2) * CAP + rank

    came = back.at[pl.ds(0, CHIPS - 1)]
    pltpu.make_async_copy(came, came, back_recv).wait()
    turned = jnp.transpose(back[...])[: 2 * CAP, :]
    found = jnp.zeros((2 * CAP, ROWS), jnp.float32)
    for part in split3(turned):
        found = found + jnp.dot(part, at_chip, preferred_element_type=jnp.float32)
    out_ref[...] = jnp.sum(jnp.where(at_lane, found, 0.0), axis=0, keepdims=True)

    gone = send.at[pl.ds(CAP, SLOTS - CAP)]
    pltpu.make_async_copy(gone, gone, send_sem).wait()
    pltpu.make_async_copy(came, came, back_send).wait()


def shards(embeddings, cluster_ids):
    anywhere = pl.BlockSpec(memory_space=pltpu.HBM)
    density = pl.pallas_call(
        kernel,
        out_shape=jax.ShapeDtypeStruct((1, ROWS), jnp.float32),
        in_specs=[anywhere, anywhere],
        out_specs=pl.BlockSpec(memory_space=pltpu.VMEM),
        scratch_shapes=[
            pltpu.VMEM((ROWS, WIDTH), jnp.float32),
            pltpu.VMEM((1, ROWS), jnp.int32),
            pltpu.VMEM((ROWS, WIDTH), jnp.bfloat16),
            pltpu.VMEM((SLOTS, WIDTH), jnp.bfloat16),
            pltpu.VMEM((SLOTS, WIDTH), jnp.bfloat16),
            pltpu.VMEM((SLOTS, 128), jnp.float32),
            pltpu.VMEM((8, SLOTS), jnp.float32),
            pltpu.VMEM((SLOTS, 128), jnp.float32),
            pltpu.VMEM((2, CHUNKS, 8, 128), jnp.float32),
            pltpu.VMEM((CHUNKS, 8, 128), jnp.float32),
            pltpu.VMEM((CHIPS, 128), jnp.float32),
            pltpu.VMEM((CHIPS, 128), jnp.float32),
            pltpu.SemaphoreType.DMA((4,)),
            pltpu.SemaphoreType.DMA,
            pltpu.SemaphoreType.DMA,
            pltpu.SemaphoreType.DMA((len(GROUPS),)),
            pltpu.SemaphoreType.DMA,
            pltpu.SemaphoreType.DMA,
            pltpu.SemaphoreType.DMA,
            pltpu.SemaphoreType.DMA,
        ],
        compiler_params=pltpu.CompilerParams(
            collective_id=0, has_side_effects=True, vmem_limit_bytes=55228 << 10
        ),
        name="density",
    )(embeddings, cluster_ids.reshape(1, ROWS))
    return density.reshape(ROWS)


def solution(mesh):
    placed = (P(("pool", "blk"), None), P(("pool", "blk"), None))
    return jax.shard_map(
        shards, mesh=mesh, in_specs=placed, out_specs=P(("pool", "blk")), check_vma=False
    )
```
